512 devices in a mesh: section: 8 (over x, core), fsdp: 32 (over y_lo, z), tile: 2 (over y_hi).
Axes of the slice: x: 4, y: 8 (y_hi: 2, y_lo: 4; y = y_hi * 4 + y_lo), z: 8, core: 2. Of those that a mesh axis runs over, the one named last changes fastest.
Arguments:
- features: bfloat16 [4, 8192, 320], P(None, ('fsdp', 'tile')), may hold values from -6 to 6
- labels: int32 [4, 8192], P(None, ('fsdp', 'tile')), may hold values from 0 to 4
- w_expand: bfloat16 [8, 320, 1280], P('section', None, 'fsdp'), may hold values from -0.3125 to 0.3125
- w_reduce: bfloat16 [8, 320, 1280], P('section', None, 'fsdp'), may hold values from -0.15625 to 0.15625
- head_weight: bfloat16 [320, 5], replicated, may hold values from -0.3125 to 0.3125
Outputs:
- grad_expand: float32 [8, 320, 1280], P('section', None, 'fsdp')
- grad_reduce: float32 [8, 320, 1280], P('section', None, 'fsdp')
The draws below stay inside these ranges and needn't reach their ends.
All inputs are finite; a program needn't handle non-finite values.
Results may differ from the reference program's by a relative error of at most 0.01.
Values may be sent and summed in bfloat16 or wider, within the bound.
A program may use at most 64 MiB of HBM per device.

```python
import math
import jax
import jax.numpy as jnp
from jax import lax

CH = 320
HID = 1280
CLASSES = 5
MICRO = 4
ROWS = 8192
SECTIONS = 8


def touch_ends(result, stream_key, low, top_value):
    longest = result.shape.index(max(result.shape))
    spots = []
    for shift in (0, 1):
        where = [jax.random.randint(jax.random.fold_in(stream_key, axis), (), 0, length) for axis, length in enumerate(result.shape)]
        where[longest] = (where[longest] + shift) % result.shape[longest]
        spots.append(tuple(where))
    return result.at[spots[0]].set(low).at[spots[1]].set(top_value)


def block_levels(own_key, shape, pieces, least, high):
    def one(dim, shards_of):
        draws = jax.random.uniform(jax.random.fold_in(jax.random.fold_in(own_key, 6), dim), (shards_of,), jnp.float32, least / len(pieces), high / len(pieces))
        return jnp.repeat(jnp.exp(draws), shape[dim] // shards_of).reshape((-1,) + (1,) * (len(shape) - dim - 1))

    factor_of = one(*pieces[0])
    for cut in pieces[1:]:
        factor_of = factor_of * one(*cut)
    return factor_of


def gaussian(own_key, shape, scale, most, cuts=(), held_as=jnp.bfloat16):
    result = scale * jax.random.normal(own_key, shape, jnp.float32)
    if cuts:
        result = result * block_levels(own_key, shape, cuts, -0.22, 0.18)
    return jnp.clip(result, -most, most).astype(held_as)


def setup_inputs(seed: int = 0) -> dict:
    splits = jax.random.split(jax.random.key(seed), 6)
    return {
        "features": gaussian(splits[0], (MICRO, ROWS, CH), 1.0, 6.0, ((1, 64),)),
        "labels": touch_ends(jax.random.randint(splits[1], (MICRO, ROWS), 0, CLASSES), jax.random.fold_in(splits[1], 1), 0, CLASSES - 1).astype(jnp.int32),
        "w_expand": gaussian(splits[2], (SECTIONS, CH, HID), CH ** -0.5, 0.3125, ((0, 8), (2, 32))),
        "w_reduce": gaussian(splits[3], (SECTIONS, CH, HID), HID ** -0.5, 0.15625, ((0, 8), (2, 32))),
        "head_weight": gaussian(splits[4], (CH, CLASSES), CH ** -0.5, 0.3125),
    }


norm_eps = 1e-06

def normalize(values):
    floats = values.astype(jnp.float32)
    centred = floats - lax.optimization_barrier(jnp.mean(floats, axis=-1, keepdims=True))
    inverse_std = lax.rsqrt(lax.optimization_barrier(jnp.mean(centred * centred, axis=-1, keepdims=True)) + norm_eps)
    return (centred * inverse_std, inverse_std)

def norm_back(values, grad_norm):
    unit, inverse_std = normalize(values)
    centred_grad = grad_norm - lax.optimization_barrier(jnp.mean(grad_norm, axis=-1, keepdims=True))
    return inverse_std * (centred_grad - unit * lax.optimization_barrier(jnp.mean(grad_norm * unit, axis=-1, keepdims=True)))

def section_forward(inputs, w_up, w_down):
    unit, _ = normalize(inputs)
    normed = unit.astype(jnp.bfloat16)
    hidden_pre = jnp.dot(normed, w_up, preferred_element_type=jnp.float32)
    hidden = jax.nn.gelu(hidden_pre).astype(jnp.bfloat16)
    branch = lax.dot_general(hidden, w_down, (((1,), (1,)), ((), ())), preferred_element_type=jnp.float32)
    return ((inputs.astype(jnp.float32) + branch).astype(jnp.bfloat16), hidden_pre)

def section_backward(inputs, hidden_pre, grad_out, w_up, w_down):
    unit, _ = normalize(inputs)
    normed = unit.astype(jnp.bfloat16)
    hidden = jax.nn.gelu(hidden_pre).astype(jnp.bfloat16)
    grad_down = lax.dot_general(grad_out, hidden, (((0,), (0,)), ((), ())), preferred_element_type=jnp.float32)
    grad_hidden = jnp.dot(grad_out, w_down, preferred_element_type=jnp.float32)
    grad_pre = jax.vjp(jax.nn.gelu, hidden_pre)[1](grad_hidden)[0].astype(jnp.bfloat16)
    grad_up = lax.dot_general(normed, grad_pre, (((0,), (0,)), ((), ())), preferred_element_type=jnp.float32)
    grad_norm = lax.dot_general(grad_pre, w_up, (((1,), (1,)), ((), ())), preferred_element_type=jnp.float32)
    grad_in = (grad_out.astype(jnp.float32) + norm_back(inputs, grad_norm)).astype(jnp.bfloat16)
    return (grad_up, grad_down, grad_in)

def head_backward(outputs, pixel_labels, head_weight, loss_scale):
    unit, _ = normalize(outputs)
    normed = unit.astype(jnp.bfloat16)
    logits = jnp.dot(normed, head_weight, preferred_element_type=jnp.float32)
    exponent = jnp.exp(logits)
    probs = exponent / lax.optimization_barrier(jnp.sum(exponent, axis=-1, keepdims=True))
    classes = lax.broadcasted_iota(jnp.int32, logits.shape, 1)
    onehot = (classes == pixel_labels[:, None]).astype(jnp.float32)
    grad_logits = ((probs - onehot) * loss_scale).astype(jnp.bfloat16)
    grad_norm = lax.dot_general(grad_logits, head_weight, (((1,), (1,)), ((), ())), preferred_element_type=jnp.float32)
    return norm_back(outputs, grad_norm).astype(jnp.bfloat16)

def reference(features, labels, w_expand, w_reduce, head_weight):
    loss_scale = 1.0 / math.sqrt(MICRO * ROWS)
    up_sums = [jnp.zeros((CH, HID), jnp.float32) for index in range(SECTIONS)]
    down_sums = [jnp.zeros((CH, HID), jnp.float32) for index in range(SECTIONS)]
    for micro_index in range(MICRO):
        current = features[micro_index]
        saved_inputs = []
        saved_pre = []
        for section_number in range(SECTIONS):
            saved_inputs.append(current)
            current, hidden_pre = section_forward(current, w_expand[section_number], w_reduce[section_number])
            saved_pre.append(hidden_pre)
        grad_out = head_backward(current, labels[micro_index], head_weight, loss_scale)
        for section_number in reversed(range(SECTIONS)):
            grad_up, grad_down, grad_out = section_backward(saved_inputs[section_number], saved_pre[section_number], grad_out, w_expand[section_number], w_reduce[section_number])
            up_sums[section_number] = up_sums[section_number] + grad_up
            down_sums[section_number] = down_sums[section_number] + grad_down
    return (jnp.stack(up_sums), jnp.stack(down_sums))
```

```python
import math

import jax
import jax.numpy as jnp
from jax import lax
from jax.experimental import pallas as pl
from jax.experimental.pallas import tpu as pltpu
from jax.sharding import PartitionSpec as P

norm_eps = 1e-06
RING = 8
LANES = 128
PACK = 208
HALF = 112
GELU_C = math.sqrt(2.0 / math.pi)
GELU_A = 0.044715
bf16 = jnp.bfloat16
f32 = jnp.float32


def nt(lhs, rhs):
    return lax.dot_general(lhs, rhs, (((1,), (1,)), ((), ())), preferred_element_type=f32)


def nn(lhs, rhs):
    return jnp.dot(lhs, rhs, preferred_element_type=f32)


def tn(lhs, rhs):
    return lax.dot_general(lhs, rhs, (((0,), (0,)), ((), ())), preferred_element_type=f32)


def eye(size):
    row = lax.broadcasted_iota(jnp.int32, (size, size), 0)
    column = lax.broadcasted_iota(jnp.int32, (size, size), 1)
    return jnp.where(row == column, 1.0, 0.0).astype(bf16)


def normalize(values):
    floats = values.astype(f32)
    centred = floats - jnp.mean(floats, axis=0, keepdims=True)
    inverse_std = lax.rsqrt(jnp.mean(centred * centred, axis=0, keepdims=True) + norm_eps)
    return centred * inverse_std, inverse_std


def norm_back(unit, inverse_std, grad):
    centred = grad - jnp.mean(grad, axis=0, keepdims=True)
    return inverse_std * (centred - unit * jnp.mean(grad * unit, axis=0, keepdims=True))


def low_pad(rows):
    return jnp.concatenate([rows, jnp.zeros_like(rows)], axis=0)


def high_pad(rows):
    return jnp.concatenate([jnp.zeros_like(rows), rows], axis=0)


def remote(src, dst, send_sem, recv_sem, device):
    return pltpu.make_async_remote_copy(
        src_ref=src,
        dst_ref=dst,
        send_sem=send_sem,
        recv_sem=recv_sem,
        device_id=device,
        device_id_type=pl.DeviceIdType.MESH,
    )


def kernel(
    sections, groups, tiles, micro, loss_scale,
    feat, labels, wup, wdown, head,
    up_out, down_out,
    gathered, up_t, down_t, mix_t, up_n, down_n, head_pad,
    xbuf, obuf, nbuf, ubuf, istd, pre, hid, gpre, dybuf, dsend,
    parts, ry, rh, qbuf, rz, tbuf, rt,
    gy_s, gz_s, g_r, fs, fr, bs, br, rys, ryr, rhs_, rhr, rzs, rzr, ts, tr,
):
    s = lax.axis_index("section")
    f = lax.axis_index("fsdp")
    t = lax.axis_index("tile")
    y_low, z = f // RING, f % RING
    height = groups * tiles
    y = t * groups + y_low
    last = sections - 1
    block = 40 * RING

    def at(y_new, z_new):
        y_new = (y_new + 2 * height) % height
        z_new = (z_new + 2 * RING) % RING
        return {"fsdp": (y_new % groups) * RING + z_new, "tile": y_new // groups}

    barrier = pltpu.get_barrier_semaphore()
    partners = [at(y, z + d) for d in range(1, RING)]
    if groups == 4:
        partners += [at(y + d, z) for d in (1, -1, 2, -2)]
    if tiles == 2:
        partners.append(at(y + groups, z))
    for device in partners:
        pl.semaphore_signal(barrier, inc=1, device_id=device, device_id_type=pl.DeviceIdType.MESH)

    @pl.when(s > 0)
    def _():
        pl.semaphore_signal(
            barrier, inc=1, device_id={"section": s - 1}, device_id_type=pl.DeviceIdType.MESH
        )

    @pl.when(s < last)
    def _():
        pl.semaphore_signal(
            barrier, inc=1, device_id={"section": s + 1}, device_id_type=pl.DeviceIdType.MESH
        )

    up_w, down_w = wup[0], wdown[0]
    stacked = jnp.concatenate([up_w[:256], down_w[:256], up_w[256:], down_w[256:]], axis=0)
    own = nt(eye(40), stacked)
    pieces = [own[:, LANES * i : LANES * (i + 1)] for i in range(5)]
    pieces.append(jnp.zeros((8, LANES), f32))
    gathered[f] = jnp.concatenate(pieces, axis=0).astype(bf16)

    pl.semaphore_wait(
        barrier,
        len(partners) + jnp.where(s > 0, 1, 0) + jnp.where(s < last, 1, 0),
    )

    def slot(j, dz):
        return ((y_low + j) % groups) * RING + (z + dz + 2 * RING) % RING

    order = (0, 1, 3, 2) if groups == 4 else (0,)
    pending = []
    if groups == 4:
        ysends = [
            remote(gathered.at[f], gathered.at[f], gy_s.at[0], g_r.at[f, 0], at(y + 1, z)),
            remote(gathered.at[f], gathered.at[f], gy_s.at[1], g_r.at[f, 0], at(y - 1, z)),
            remote(
                gathered.at[f, pl.ds(0, HALF)], gathered.at[f, pl.ds(0, HALF)],
                gy_s.at[2], g_r.at[f, 0], at(y + 2, z),
            ),
            remote(
                gathered.at[f, pl.ds(HALF, PACK - HALF)], gathered.at[f, pl.ds(HALF, PACK - HALF)],
                gy_s.at[3], g_r.at[f, 1], at(y - 2, z),
            ),
        ]
        for copy in ysends:
            copy.start()
        pending += ysends

    def arrived(index):
        remote(
            gathered.at[index], gathered.at[index], gy_s.at[0], g_r.at[index, 0], at(y, z + 1)
        ).wait_recv()

    def ysend_arrived(index):
        remote(
            gathered.at[index, pl.ds(0, HALF)], gathered.at[index, pl.ds(0, HALF)],
            gy_s.at[2], g_r.at[index, 0], at(y, z + 1),
        ).wait_recv()
        remote(
            gathered.at[index, pl.ds(HALF, PACK - HALF)], gathered.at[index, pl.ds(HALF, PACK - HALF)],
            gy_s.at[3], g_r.at[index, 1], at(y, z + 1),
        ).wait_recv()

    far = RING // 2
    count = 0
    for step in range(1, far + 1):
        for place, j in enumerate(order):
            if step == 1:
                if j == 2:
                    ysend_arrived(slot(j, 0))
                elif j:
                    arrived(slot(j, 0))
            early = place < (len(order) + 1) // 2
            for side in (1, -1):
                index = slot(j, -side * (step - 1))
                if step > 1:
                    arrived(index)
                if step == far and early != (side == 1):
                    continue
                copy = remote(
                    gathered.at[index], gathered.at[index],
                    gz_s.at[count], g_r.at[index, 0], at(y, z + side),
                )
                copy.start()
                pending.append(copy)
                count += 1
    for j in order:
        arrived(slot(j, far))

    def unpack(pair, carry):
        first = gathered[2 * pair].astype(f32)
        second = gathered[2 * pair + 1].astype(f32)
        rows = pl.ds(pl.multiple_of(pair * 80, 16), 80)

        def both(i):
            return jnp.concatenate(
                [first[40 * i : 40 * i + 40], second[40 * i : 40 * i + 40]], axis=0
            ).astype(bf16)

        up_t[rows, 0:128] = both(0)
        up_t[rows, 128:256] = both(1)
        down_t[rows, 0:128] = both(2)
        down_t[rows, 128:256] = both(3)
        mix_t[rows, :] = both(4)
        return carry

    lax.fori_loop(0, groups * RING // 2, unpack, 0)
    wide = eye(256)
    down_n[0:256, :] = nt(wide, down_t[...]).astype(bf16)
    turned = nt(eye(128), mix_t[...]).astype(bf16)
    down_n[256:320, :] = turned[64:128]

    @pl.when(s > 0)
    def _():
        up_n[0:256, :] = nt(wide, up_t[...]).astype(bf16)
        up_n[256:320, :] = turned[0:64]

    @pl.when(s == 0)
    def _():
        for m in range(micro):
            xbuf[m] = nt(eye(320), feat[m]).astype(bf16)

    @pl.when(s == last)
    def _():
        head_pad[...] = jnp.zeros_like(head_pad)
        head_pad[:, 0:5] = head[...]

    def forward(m, carry):
        @pl.when(s > 0)
        def _():
            remote(obuf.at[m], xbuf.at[m], fs.at[m], fr.at[m], {"section": s}).wait_recv()

        x = xbuf[m]
        unit, inverse_std = normalize(x)
        normed = unit.astype(bf16)
        ubuf[m] = unit
        istd[m] = inverse_std
        nbuf[m] = normed
        low, high = normed[:256], low_pad(normed[256:])
        total = x.astype(f32)
        for g in range(groups):
            rows = slice(block * g, block * (g + 1))
            before = nn(up_t[rows, :], low) + nn(mix_t[rows, :], high)
            pre[m, rows, :] = before
            bent = jnp.tanh(GELU_C * (before + GELU_A * (before * before * before)))
            hidden = (before * (0.5 * (1.0 + bent))).astype(bf16)
            hid[m, rows, :] = hidden
        out = (total + nn(down_n[...], hid[m])).astype(bf16)
        obuf[m] = out

        @pl.when(s < last)
        def _():
            remote(obuf.at[m], xbuf.at[m], fs.at[m], fr.at[m], {"section": s + 1}).start()

        @pl.when(s == last)
        def _():
            head_unit, head_istd = normalize(obuf[m])
            logits = tn(head_pad[...], head_unit.astype(bf16))[0:8]
            classes = lax.broadcasted_iota(jnp.int32, logits.shape, 0)
            exponent = jnp.where(classes < 5, jnp.exp(logits), 0.0)
            probs = exponent / jnp.sum(exponent, axis=0, keepdims=True)
            onehot = jnp.where(classes == labels[pl.ds(m, 1), :], 1.0, 0.0)
            grad_logits = (probs - onehot) * loss_scale
            grad_logits = jnp.concatenate(
                [grad_logits, jnp.zeros((LANES - 8, LANES), f32)], axis=0
            ).astype(bf16)
            grad_norm = nn(head_pad[...], grad_logits)
            dybuf[m] = norm_back(head_unit, head_istd, grad_norm).astype(bf16)

        return carry

    lax.fori_loop(0, micro, forward, 0)

    def backward(m, carry):
        @pl.when(s < last)
        def _():
            remote(dsend.at[m], dybuf.at[m], bs.at[m], br.at[m], {"section": s}).wait_recv()

        dy = dybuf[m]
        low, high = dy[:256], high_pad(dy[256:])
        for g in range(groups):
            rows = slice(block * g, block * (g + 1))
            grad_hidden = nn(down_t[rows, :], low) + nn(mix_t[rows, :], high)
            before = pre[m, rows, :]
            square = before * before
            bent = jnp.tanh(GELU_C * (before + GELU_A * (square * before)))
            slope = 0.5 * (1.0 + bent) + (0.5 * before) * (1.0 - bent * bent) * (
                GELU_C * (1.0 + (3.0 * GELU_A) * square)
            )
            gpre[m, rows, :] = (grad_hidden * slope).astype(bf16)

        @pl.when(s > 0)
        def _():
            grad_norm = nn(up_n[...], gpre[m])
            grad_in = dybuf[m].astype(f32) + norm_back(ubuf[m], istd[m], grad_norm)
            dsend[m] = grad_in.astype(bf16)
            remote(dsend.at[m], dybuf.at[m], bs.at[m], br.at[m], {"section": s - 1}).start()

        return carry

    lax.fori_loop(0, micro, backward, 0)

    normed = jnp.concatenate([nbuf[m] for m in range(micro)], axis=1)
    grads = jnp.concatenate([dybuf[m] for m in range(micro)], axis=1)
    normed_low, normed_high = normed[:256], low_pad(normed[256:])
    grads_low, grads_high = grads[:256], high_pad(grads[256:])

    def weight_grads(g):
        rows = pl.ds(pl.multiple_of(g * block, 16), block)
        grad_pre = jnp.concatenate([gpre[m, rows, :] for m in range(micro)], axis=1)
        hidden = jnp.concatenate([hid[m, rows, :] for m in range(micro)], axis=1)
        up = nt(grad_pre, normed_low)
        down = nt(hidden, grads_low)
        mix = nt(grad_pre, normed_high) + nt(hidden, grads_high)
        for k in range(RING):
            r = slice(40 * k, 40 * k + 40)
            parts[g, k] = jnp.concatenate(
                [up[r, :128], up[r, 128:], down[r, :128], down[r, 128:], mix[r],
                 jnp.zeros((8, LANES), f32)], axis=0,
            ).astype(bf16)

    half = RING // 2
    rsends = []
    if groups == 4:
        g = (y_low + 2) % groups
        weight_grads(g)
        rsends += [
            remote(parts.at[g, pl.ds(0, half)], rh.at[0], rhs_.at[0], rhr.at[0], at(y - 2, z)),
            remote(parts.at[g, pl.ds(half, half)], rh.at[1], rhs_.at[1], rhr.at[1], at(y + 2, z)),
        ]
        rsends[0].start()
        rsends[1].start()
        for i, d in enumerate((1, -1)):
            g = (y_low + d + groups) % groups
            weight_grads(g)
            copy = remote(parts.at[g], ry.at[i], rys.at[i], ryr.at[i], at(y + d, z))
            copy.start()
            rsends.append(copy)
    weight_grads(y_low)
    for copy in rsends:
        copy.wait_recv()

    def group_sum(k):
        total = parts[y_low, k].astype(f32)
        if groups == 4:
            total += ry[0, k].astype(f32) + ry[1, k].astype(f32)
            total += rh[k // half, k % half].astype(f32)
        return total

    zsends = []
    for d in [half] + [e for i in range(1, half) for e in (half - i, half + i)]:
        k = (z + d) % RING
        qbuf[k] = group_sum(k).astype(bf16)
        copy = remote(qbuf.at[k], rz.at[d - 1], rzs.at[d - 1], rzr.at[d - 1], at(y, z + d))
        copy.start()
        zsends.append(copy)
    result = group_sum(z)
    for d in range(1, RING):
        zsends[d - 1].wait_recv()
    for d in range(1, RING):
        result += rz[d - 1].astype(f32)
    if tiles == 2:
        rounded = result.astype(bf16)
        tbuf[...] = rounded
        tsend = remote(tbuf, rt, ts.at[0], tr.at[0], at(y + groups, z))
        tsend.start()
        tsend.wait_recv()
        result = rounded.astype(f32) + rt[...].astype(f32)
    up_out[:, 0:128] = result[0:40]
    up_out[:, 128:256] = result[40:80]
    up_out[:, 256:320] = result[160:200, 0:64]
    down_out[:, 0:128] = result[80:120]
    down_out[:, 128:256] = result[120:160]
    down_out[:, 256:320] = result[160:200, 64:128]

    for copy in pending + rsends + zsends:
        copy.wait_send()
    if tiles == 2:
        tsend.wait_send()

    @pl.when(s < last)
    def _():
        for m in range(micro):
            remote(obuf.at[m], xbuf.at[m], fs.at[m], fr.at[m], {"section": s + 1}).wait_send()

    @pl.when(s > 0)
    def _():
        for m in range(micro):
            remote(dsend.at[m], dybuf.at[m], bs.at[m], br.at[m], {"section": s - 1}).wait_send()


def local(features, labels, w_expand, w_reduce, head_weight):
    sections, shards, tiles = (lax.axis_size(a) for a in ("section", "fsdp", "tile"))
    groups = shards // RING
    micro, rows, width = features.shape
    hidden = 40 * shards
    loss_scale = 1.0 / math.sqrt(micro * rows * shards * tiles)
    vmem, dma = pltpu.VMEM, pltpu.SemaphoreType.DMA
    half = RING // 2

    def body(*refs):
        kernel(sections, groups, tiles, micro, loss_scale, *refs)

    up, down = pl.pallas_call(
        body,
        out_shape=[jax.ShapeDtypeStruct((40, width), f32)] * 2,
        in_specs=[pl.BlockSpec(memory_space=pltpu.VMEM)] * 5,
        out_specs=[pl.BlockSpec(memory_space=pltpu.VMEM)] * 2,
        scratch_shapes=[
            vmem((shards, PACK, LANES), bf16),
            vmem((hidden, 256), bf16),
            vmem((hidden, 256), bf16),
            vmem((hidden, LANES), bf16),
            vmem((width, hidden), bf16),
            vmem((width, hidden), bf16),
            vmem((width, LANES), bf16),
            vmem((micro, width, rows), bf16),
            vmem((micro, width, rows), bf16),
            vmem((micro, width, rows), bf16),
            vmem((micro, width, rows), f32),
            vmem((micro, 1, rows), f32),
            vmem((micro, hidden, rows), f32),
            vmem((micro, hidden, rows), bf16),
            vmem((micro, hidden, rows), bf16),
            vmem((micro, width, rows), bf16),
            vmem((micro, width, rows), bf16),
            vmem((groups, RING, PACK, LANES), bf16),
            vmem((2, RING, PACK, LANES), bf16),
            vmem((2, half, PACK, LANES), bf16),
            vmem((RING, PACK, LANES), bf16),
            vmem((RING - 1, PACK, LANES), bf16),
            vmem((PACK, LANES), bf16),
            vmem((PACK, LANES), bf16),
            dma((4,)),
            dma((groups * RING,)),
            dma((shards, 2)),
            dma((micro,)),
            dma((micro,)),
            dma((micro,)),
            dma((micro,)),
            dma((2,)),
            dma((2,)),
            dma((2,)),
            dma((2,)),
            dma((RING - 1,)),
            dma((RING - 1,)),
            dma((1,)),
            dma((1,)),
        ],
        compiler_params=pltpu.CompilerParams(
            collective_id=0, has_side_effects=True, vmem_limit_bytes=48 * 1024 * 1024
        ),
    )(features, labels, w_expand, w_reduce, head_weight)
    return up.T[None], down.T[None]


def solution(mesh):
    return jax.shard_map(
        local,
        mesh=mesh,
        in_specs=(
            P(None, ("fsdp", "tile"), None),
            P(None, ("fsdp", "tile")),
            P("section", None, "fsdp"),
            P("section", None, "fsdp"),
            P(),
        ),
        out_specs=(P("section", None, "fsdp"), P("section", None, "fsdp")),
        check_vma=False,
    )
```

```python
import math

import jax
import jax.numpy as jnp
from jax import lax
from jax.experimental import pallas as pl
from jax.experimental.pallas import tpu as pltpu
from jax.sharding import PartitionSpec as P

norm_eps = 1e-06
RING = 8
LANES = 128
PACK = 208
HALF = 112
FIRST = 1
GELU_C = math.sqrt(2.0 / math.pi)
GELU_A = 0.044715
bf16 = jnp.bfloat16
f32 = jnp.float32


def nt(lhs, rhs):
    return lax.dot_general(lhs, rhs, (((1,), (1,)), ((), ())), preferred_element_type=f32)


def nn(lhs, rhs):
    return jnp.dot(lhs, rhs, preferred_element_type=f32)


def eye(size):
    row = lax.broadcasted_iota(jnp.int32, (size, size), 0)
    column = lax.broadcasted_iota(jnp.int32, (size, size), 1)
    return jnp.where(row == column, 1.0, 0.0).astype(bf16)


def place(shift):
    row = lax.broadcasted_iota(jnp.int32, (LANES, 64), 0)
    column = lax.broadcasted_iota(jnp.int32, (LANES, 64), 1)
    return jnp.where(row == column + shift, 1.0, 0.0).astype(bf16)


def normalize(values):
    floats = values.astype(f32)
    centred = floats - jnp.mean(floats, axis=0, keepdims=True)
    inverse_std = lax.rsqrt(jnp.mean(centred * centred, axis=0, keepdims=True) + norm_eps)
    return centred * inverse_std, inverse_std


def norm_back(unit, inverse_std, grad):
    centred = grad - jnp.mean(grad, axis=0, keepdims=True)
    return inverse_std * (centred - unit * jnp.mean(grad * unit, axis=0, keepdims=True))


def low_pad(rows):
    return jnp.concatenate([rows, jnp.zeros_like(rows)], axis=0)


def high_pad(rows):
    return jnp.concatenate([jnp.zeros_like(rows), rows], axis=0)


def remote(src, dst, send_sem, recv_sem, device):
    return pltpu.make_async_remote_copy(
        src_ref=src,
        dst_ref=dst,
        send_sem=send_sem,
        recv_sem=recv_sem,
        device_id=device,
        device_id_type=pl.DeviceIdType.MESH,
    )


def kernel(
    sections, groups, tiles, micro, loss_scale,
    feat_any, labels_any, wup_any, wdown_any, head_any,
    up_out, down_out,
    feat, labels, wup, wdown, head, gathered, up_t, down_t, mix_t, up_n, down_n, head_pad, head_n,
    xbuf, obuf, nbuf, ubuf, istd, pre, hid, gpre, dybuf, dsend,
    parts, ry, rh, qbuf, rz, tbuf, rt, za, ysum, yall,
    in_sem, g_s, g_r, fs, fr, bs, br, rys, ryr, rhs_, rhr, rzs, rzr, ts, tr, zs, zr, ys, yr,
):
    s = lax.axis_index("section")
    f = lax.axis_index("fsdp")
    t = lax.axis_index("tile")
    y_low, z = f // RING, f % RING
    height = groups * tiles
    y = t * groups + y_low
    last = sections - 1
    block = 40 * RING

    def at(y_new, z_new):
        y_new = (y_new + 2 * height) % height
        z_new = (z_new + 2 * RING) % RING
        return {"fsdp": (y_new % groups) * RING + z_new, "tile": y_new // groups}

    copies_in = [
        pltpu.make_async_copy(source, target, in_sem.at[i])
        for i, (source, target) in enumerate(
            ((wup_any, wup), (wdown_any, wdown), (feat_any, feat), (labels_any, labels), (head_any, head))
        )
    ]
    for copy in copies_in:
        copy.start()

    barrier = pltpu.get_barrier_semaphore()
    partners = [at(y, z + d) for d in range(1, RING)]
    partners += [at(y + d, z) for d in range(1, height)]
    for device in partners:
        pl.semaphore_signal(barrier, inc=1, device_id=device, device_id_type=pl.DeviceIdType.MESH)

    @pl.when(s > 0)
    def _():
        pl.semaphore_signal(
            barrier, inc=1, device_id={"section": s - 1}, device_id_type=pl.DeviceIdType.MESH
        )

    @pl.when(s < last)
    def _():
        pl.semaphore_signal(
            barrier, inc=1, device_id={"section": s + 1}, device_id_type=pl.DeviceIdType.MESH
        )

    for copy in copies_in[:2]:
        copy.wait()
    up_w, down_w = wup[...], wdown[...]
    mixed = nt(up_w[:, 256:], place(0)) + nt(down_w[:, 256:], place(64))
    pieces = [up_w[:, :128], up_w[:, 128:256], down_w[:, :128], down_w[:, 128:256]]
    pieces = [piece.astype(f32) for piece in pieces] + [mixed, jnp.zeros((8, LANES), f32)]
    gathered[f] = jnp.concatenate(pieces, axis=0).astype(bf16)

    pl.semaphore_wait(
        barrier,
        len(partners) + jnp.where(s > 0, 1, 0) + jnp.where(s < last, 1, 0),
    )

    def slot(j, dz):
        return ((y_low + j) % groups) * RING + (z + dz + 2 * RING) % RING

    order = (0, 1, 3, 2) if groups == 4 else (0,)
    far = RING // 2
    low_rows, high_rows = pl.ds(0, HALF), pl.ds(HALF, PACK - HALF)
    is_a = s % 2 == FIRST

    def arrived(index):
        remote(
            gathered.at[index], gathered.at[index], g_s.at[0], g_r.at[index, 0], at(y, z + 1)
        ).wait_recv()

    def halves_arrived(index):
        for i, rows in enumerate((low_rows, high_rows)):
            remote(
                gathered.at[index, rows], gathered.at[index, rows],
                g_s.at[0], g_r.at[index, i], at(y, z + 1),
            ).wait_recv()

    def y_sends(index, first):
        if groups != 4:
            return []
        copies = [
            remote(gathered.at[index], gathered.at[index], g_s.at[first], g_r.at[index, 0], at(y + 1, z)),
            remote(gathered.at[index], gathered.at[index], g_s.at[first + 1], g_r.at[index, 0], at(y - 1, z)),
            remote(
                gathered.at[index, low_rows], gathered.at[index, low_rows],
                g_s.at[first + 2], g_r.at[index, 0], at(y + 2, z),
            ),
            remote(
                gathered.at[index, high_rows], gathered.at[index, high_rows],
                g_s.at[first + 3], g_r.at[index, 1], at(y - 2, z),
            ),
        ]
        for copy in copies:
            copy.start()
        return copies

    @pl.when(is_a)
    def _():
        sent = y_sends(f, 0)

        def z_send(index, d):
            copy = remote(
                gathered.at[index], gathered.at[index],
                g_s.at[len(sent)], g_r.at[index, 0], at(y, z + d),
            )
            copy.start()
            sent.append(copy)

        for j in order:
            if j:
                (halves_arrived if j == 2 else arrived)(slot(j, 0))
            for d in range(1, min(far, 2) + 1):
                for side in (1, -1):
                    if d == far and (j in order[: (len(order) + 1) // 2]) != (side == 1):
                        continue
                    z_send(slot(j, 0), side * d)
        for step in range(2, far + 1):
            for j in order:
                early = j in order[: (len(order) + 1) // 2]
                for side in (1, -1):
                    index = slot(j, -side * (step - 1))
                    arrived(index)
                    if step < 3 or (step == far and early != (side == 1)):
                        continue
                    z_send(index, side)
        for j in order:
            arrived(slot(j, far))
        for copy in sent:
            copy.wait_send()

    near_first = [d for i in range(1, far) for d in (i, -i)] + [far]

    @pl.when(jnp.logical_not(is_a))
    def _():
        sent = []
        for i, d in enumerate(near_first):
            copy = remote(gathered.at[f], gathered.at[f], g_s.at[i], g_r.at[f, 0], at(y, z + d))
            copy.start()
            sent.append(copy)
        sent += y_sends(f, len(sent))
        for d in near_first:
            arrived(slot(0, d))
            sent += y_sends(slot(0, d), len(sent))
        if groups == 4:
            for d in [0] + near_first:
                arrived(slot(1, d))
                arrived(slot(3, d))
                halves_arrived(slot(2, d))
        for copy in sent:
            copy.wait_send()

    for copy in copies_in[2:]:
        copy.wait()

    def unpack(pair, carry):
        first = gathered[2 * pair].astype(f32)
        second = gathered[2 * pair + 1].astype(f32)
        rows = pl.ds(pl.multiple_of(pair * 80, 16), 80)

        def both(i):
            return jnp.concatenate(
                [first[40 * i : 40 * i + 40], second[40 * i : 40 * i + 40]], axis=0
            ).astype(bf16)

        up_t[rows, 0:128] = both(0)
        up_t[rows, 128:256] = both(1)
        down_t[rows, 0:128] = both(2)
        down_t[rows, 128:256] = both(3)
        mix_t[rows, :] = both(4)
        return carry

    lax.fori_loop(0, groups * RING // 2, unpack, 0)
    wide = eye(256)
    down_n[0:256, :] = nt(wide, down_t[...]).astype(bf16)
    turned = nt(eye(128), mix_t[...]).astype(bf16)
    down_n[256:320, :] = turned[64:128]

    @pl.when(s > 0)
    def _():
        up_n[0:256, :] = nt(wide, up_t[...]).astype(bf16)
        up_n[256:320, :] = turned[0:64]

    @pl.when(s == 0)
    def _():
        for m in range(micro):
            xbuf[m] = feat[m]

    @pl.when(s == last)
    def _():
        head_pad[...] = jnp.zeros_like(head_pad)
        head_pad[0:5, :] = head[...]
        head_n[...] = nt(eye(320), head_pad[...]).astype(bf16)

    def forward(m, carry):
        @pl.when(s > 0)
        def _():
            remote(obuf.at[m], xbuf.at[m], fs.at[m], fr.at[m], {"section": s}).wait_recv()

        x = xbuf[m]
        unit, inverse_std = normalize(x)
        normed = unit.astype(bf16)
        ubuf[m] = unit
        istd[m] = inverse_std
        nbuf[m] = normed
        low, high = normed[:256], low_pad(normed[256:])
        total = x.astype(f32)
        for g in range(groups):
            rows = slice(block * g, block * (g + 1))
            before = nn(up_t[rows, :], low) + nn(mix_t[rows, :], high)
            pre[m, rows, :] = before
            bent = jnp.tanh(GELU_C * (before + GELU_A * (before * before * before)))
            hidden = (before * (0.5 * (1.0 + bent))).astype(bf16)
            hid[m, rows, :] = hidden
        out = (total + nn(down_n[...], hid[m])).astype(bf16)
        obuf[m] = out

        @pl.when(s < last)
        def _():
            remote(obuf.at[m], xbuf.at[m], fs.at[m], fr.at[m], {"section": s + 1}).start()

        @pl.when(s == last)
        def _():
            head_unit, head_istd = normalize(obuf[m])
            logits = nn(head_pad[0:16, :], head_unit.astype(bf16))[0:8]
            classes = lax.broadcasted_iota(jnp.int32, logits.shape, 0)
            exponent = jnp.where(classes < 5, jnp.exp(logits), 0.0)
            probs = exponent / jnp.sum(exponent, axis=0, keepdims=True)
            onehot = jnp.where(classes == labels[pl.ds(m, 1), :], 1.0, 0.0)
            grad_logits = (probs - onehot) * loss_scale
            grad_logits = jnp.concatenate(
                [grad_logits, jnp.zeros((LANES - 8, LANES), f32)], axis=0
            ).astype(bf16)
            grad_norm = nn(head_n[...], grad_logits)
            dybuf[m] = norm_back(head_unit, head_istd, grad_norm).astype(bf16)

        return carry

    lax.fori_loop(0, micro, forward, 0)

    def backward(m, carry):
        @pl.when(s < last)
        def _():
            remote(dsend.at[m], dybuf.at[m], bs.at[m], br.at[m], {"section": s}).wait_recv()

        dy = dybuf[m]
        low, high = dy[:256], high_pad(dy[256:])
        for g in range(groups):
            rows = slice(block * g, block * (g + 1))
            grad_hidden = nn(down_t[rows, :], low) + nn(mix_t[rows, :], high)
            before = pre[m, rows, :]
            square = before * before
            bent = jnp.tanh(GELU_C * (before + GELU_A * (square * before)))
            slope = 0.5 * (1.0 + bent) + (0.5 * before) * (1.0 - bent * bent) * (
                GELU_C * (1.0 + (3.0 * GELU_A) * square)
            )
            gpre[m, rows, :] = (grad_hidden * slope).astype(bf16)

        @pl.when(s > 0)
        def _():
            grad_norm = nn(up_n[...], gpre[m])
            grad_in = dybuf[m].astype(f32) + norm_back(ubuf[m], istd[m], grad_norm)
            dsend[m] = grad_in.astype(bf16)
            remote(dsend.at[m], dybuf.at[m], bs.at[m], br.at[m], {"section": s - 1}).start()

        return carry

    lax.fori_loop(0, micro, backward, 0)

    normed = jnp.concatenate([nbuf[m] for m in range(micro)], axis=1)
    grads = jnp.concatenate([dybuf[m] for m in range(micro)], axis=1)
    normed_low, normed_high = normed[:256], low_pad(normed[256:])
    grads_low, grads_high = grads[:256], high_pad(grads[256:])

    def weight_grads(g):
        rows = pl.ds(pl.multiple_of(g * block, 16), block)
        grad_pre = jnp.concatenate([gpre[m, rows, :] for m in range(micro)], axis=1)
        hidden = jnp.concatenate([hid[m, rows, :] for m in range(micro)], axis=1)
        up = nt(grad_pre, normed_low)
        down = nt(hidden, grads_low)
        mix = nt(grad_pre, normed_high) + nt(hidden, grads_high)
        for k in range(RING):
            r = slice(40 * k, 40 * k + 40)
            parts[g, k] = jnp.concatenate(
                [up[r, :128], up[r, 128:], down[r, :128], down[r, 128:], mix[r],
                 jnp.zeros((8, LANES), f32)], axis=0,
            ).astype(bf16)

    def write(result):
        up_out[:, 0:128] = result[0:40]
        up_out[:, 128:256] = result[40:80]
        up_out[:, 256:320] = result[160:200, 0:64]
        down_out[:, 0:128] = result[80:120]
        down_out[:, 128:256] = result[120:160]
        down_out[:, 256:320] = result[160:200, 64:128]

    @pl.when(is_a)
    def _():
        for g in range(groups):
            weight_grads(g)
        sent = []
        for step in range(1, far + 1):
            for where in range(groups):
                g = (y_low + where) % groups
                early = where < (groups + 1) // 2
                for i, side in enumerate((1, -1)):
                    if step == 1 and early != (side == 1):
                        continue
                    k = (z + side * (far + 1 - step) + RING) % RING
                    source = parts.at[g, k]
                    if step > 2 or (step == 2 and early == (side == 1)):
                        source = za.at[i, step - 2, where]
                        remote(source, source, zs.at[0], zr.at[i, step - 2, where], at(y, z + 1)).wait_recv()
                        source[...] = (source[...].astype(f32) + parts[g, k].astype(f32)).astype(bf16)
                    copy = remote(
                        source, za.at[i, step - 1, where],
                        zs.at[len(sent)], zr.at[i, step - 1, where], at(y, z + side),
                    )
                    copy.start()
                    sent.append(copy)
        for where in ((0, 2, 1, 3) if groups == 4 else range(groups)):
            g = (y_low + where) % groups
            early = where < (groups + 1) // 2
            total = parts[g, z].astype(f32)
            for i, side in enumerate((1, -1)):
                if far == 1 and early != (side == 1):
                    continue
                source = za.at[i, far - 1, where]
                remote(source, source, zs.at[0], zr.at[i, far - 1, where], at(y, z + 1)).wait_recv()
                total += source[...].astype(f32)
            ysum[where] = total.astype(bf16)
            for e in range(1, height):
                if e % groups == where:
                    copy = remote(ysum.at[where], yall.at[y], ys.at[e], yr.at[y], at(y + e, z))
                    copy.start()
                    sent.append(copy)
        yall[y] = ysum[0]
        for e in range(1, height):
            source = yall.at[(y + e) % height]
            remote(source, source, ys.at[0], yr.at[(y + e) % height], at(y, z + 1)).wait_recv()
        total = yall[0].astype(f32)
        for e in range(1, height):
            total += yall[e].astype(f32)
        write(total)
        for copy in sent:
            copy.wait_send()

    @pl.when(jnp.logical_not(is_a))
    def _():
        sent = []
        far_first = [far] + [d for i in range(1, far) for d in (far - i, far + i)]
        if groups == 4:
            g = (y_low + 2) % groups
            weight_grads(g)
            for d in far_first + [0]:
                k = (z + d) % RING
                copy = remote(
                    parts.at[g, k], rh.at[k], rhs_.at[d], rhr.at[k],
                    at(y + jnp.where(k < far, -2, 2), z),
                )
                copy.start()
                sent.append(copy)
            for g in ((y_low + 1) % groups, (y_low + 3) % groups):
                weight_grads(g)
            for d in far_first + [0]:
                k = (z + d) % RING
                for i, side in enumerate((1, -1)):
                    g = (y_low + side + groups) % groups
                    copy = remote(parts.at[g, k], ry.at[i, k], rys.at[i, d], ryr.at[i, k], at(y + side, z))
                    copy.start()
                    sent.append(copy)
        weight_grads(y_low)

        def group_sum(k):
            total = parts[y_low, k].astype(f32)
            if groups == 4:
                remote(rh.at[k], rh.at[k], rhs_.at[0], rhr.at[k], at(y, z + 1)).wait_recv()
                for i in range(2):
                    remote(ry.at[i, k], ry.at[i, k], rys.at[i, 0], ryr.at[i, k], at(y, z + 1)).wait_recv()
                total += ry[0, k].astype(f32) + ry[1, k].astype(f32) + rh[k].astype(f32)
            return total

        for d in far_first:
            k = (z + d) % RING
            qbuf[k] = group_sum(k).astype(bf16)
            copy = remote(qbuf.at[k], rz.at[d - 1], rzs.at[d - 1], rzr.at[d - 1], at(y, z + d))
            copy.start()
            sent.append(copy)
        result = group_sum(z)
        for d in range(1, RING):
            remote(rz.at[d - 1], rz.at[d - 1], rzs.at[0], rzr.at[d - 1], at(y, z + 1)).wait_recv()
            result += rz[d - 1].astype(f32)
        if tiles == 2:
            rounded = result.astype(bf16)
            tbuf[...] = rounded
            copy = remote(tbuf, rt, ts.at[0], tr.at[0], at(y + groups, z))
            copy.start()
            sent.append(copy)
            copy.wait_recv()
            result = rounded.astype(f32) + rt[...].astype(f32)
        write(result)
        for copy in sent:
            copy.wait_send()

    @pl.when(s < last)
    def _():
        for m in range(micro):
            remote(obuf.at[m], xbuf.at[m], fs.at[m], fr.at[m], {"section": s + 1}).wait_send()

    @pl.when(s > 0)
    def _():
        for m in range(micro):
            remote(dsend.at[m], dybuf.at[m], bs.at[m], br.at[m], {"section": s - 1}).wait_send()


def local(features, labels, w_expand, w_reduce, head_weight):
    sections, shards, tiles = (lax.axis_size(a) for a in ("section", "fsdp", "tile"))
    groups = shards // RING
    micro, rows, width = features.shape
    hidden = 40 * shards
    loss_scale = 1.0 / math.sqrt(micro * rows * shards * tiles)
    vmem, dma = pltpu.VMEM, pltpu.SemaphoreType.DMA
    half = RING // 2

    def body(*refs):
        kernel(sections, groups, tiles, micro, loss_scale, *refs)

    up, down = pl.pallas_call(
        body,
        out_shape=[jax.ShapeDtypeStruct((40, width), f32)] * 2,
        in_specs=[pl.BlockSpec(memory_space=pl.ANY)] * 5,
        out_specs=[pl.BlockSpec(memory_space=pltpu.VMEM)] * 2,
        scratch_shapes=[
            vmem((micro, width, rows), bf16),
            vmem((micro, rows), jnp.int32),
            vmem((40, width), bf16),
            vmem((40, width), bf16),
            vmem((5, width), bf16),
            vmem((shards, PACK, LANES), bf16),
            vmem((hidden, 256), bf16),
            vmem((hidden, 256), bf16),
            vmem((hidden, LANES), bf16),
            vmem((width, hidden), bf16),
            vmem((width, hidden), bf16),
            vmem((LANES, width), bf16),
            vmem((width, LANES), bf16),
            vmem((micro, width, rows), bf16),
            vmem((micro, width, rows), bf16),
            vmem((micro, width, rows), bf16),
            vmem((micro, width, rows), f32),
            vmem((micro, 1, rows), f32),
            vmem((micro, hidden, rows), f32),
            vmem((micro, hidden, rows), bf16),
            vmem((micro, hidden, rows), bf16),
            vmem((micro, width, rows), bf16),
            vmem((micro, width, rows), bf16),
            vmem((groups, RING, PACK, LANES), bf16),
            vmem((2, RING, PACK, LANES), bf16),
            vmem((RING, PACK, LANES), bf16),
            vmem((RING, PACK, LANES), bf16),
            vmem((RING - 1, PACK, LANES), bf16),
            vmem((PACK, LANES), bf16),
            vmem((PACK, LANES), bf16),
            vmem((2, half, groups, PACK, LANES), bf16),
            vmem((groups, PACK, LANES), bf16),
            vmem((groups * tiles, PACK, LANES), bf16),
            dma((5,)),
            dma((7 * RING,)),
            dma((shards, 2)),
            dma((micro,)),
            dma((micro,)),
            dma((micro,)),
            dma((micro,)),
            dma((2, RING)),
            dma((2, RING)),
            dma((RING,)),
            dma((RING,)),
            dma((RING - 1,)),
            dma((RING - 1,)),
            dma((1,)),
            dma((1,)),
            dma((groups * RING,)),
            dma((2, half, groups)),
            dma((groups * tiles,)),
            dma((groups * tiles,)),
        ],
        compiler_params=pltpu.CompilerParams(
            collective_id=0, has_side_effects=True, vmem_limit_bytes=60 * 1024 * 1024
        ),
    )(features.transpose(0, 2, 1), labels, w_expand[0].T, w_reduce[0].T, head_weight.T)
    return up.T[None], down.T[None]


def solution(mesh):
    return jax.shard_map(
        local,
        mesh=mesh,
        in_specs=(
            P(None, ("fsdp", "tile"), None),
            P(None, ("fsdp", "tile")),
            P("section", None, "fsdp"),
            P("section", None, "fsdp"),
            P(),
        ),
        out_specs=(P("section", None, "fsdp"), P("section", None, "fsdp")),
        check_vma=False,
    )
```

```python
import math

import jax
import jax.numpy as jnp
from jax import lax
from jax.experimental import pallas as pl
from jax.experimental.pallas import tpu as pltpu
from jax.sharding import PartitionSpec as P

norm_eps = 1e-06
RING = 8
LANES = 128
PACK = 208
HALF = 112
FIRST = 1
FIRST_SUM = 1
GELU_C = math.sqrt(2.0 / math.pi)
GELU_A = 0.044715
bf16 = jnp.bfloat16
f32 = jnp.float32


def nt(lhs, rhs):
    return lax.dot_general(lhs, rhs, (((1,), (1,)), ((), ())), preferred_element_type=f32)


def nn(lhs, rhs):
    return jnp.dot(lhs, rhs, preferred_element_type=f32)


def eye(size):
    row = lax.broadcasted_iota(jnp.int32, (size, size), 0)
    column = lax.broadcasted_iota(jnp.int32, (size, size), 1)
    return jnp.where(row == column, 1.0, 0.0).astype(bf16)


def place(shift):
    row = lax.broadcasted_iota(jnp.int32, (LANES, 64), 0)
    column = lax.broadcasted_iota(jnp.int32, (LANES, 64), 1)
    return jnp.where(row == column + shift, 1.0, 0.0).astype(bf16)


def normalize(values):
    floats = values.astype(f32)
    centred = floats - jnp.mean(floats, axis=0, keepdims=True)
    inverse_std = lax.rsqrt(jnp.mean(centred * centred, axis=0, keepdims=True) + norm_eps)
    return centred * inverse_std, inverse_std


def norm_back(unit, inverse_std, grad):
    centred = grad - jnp.mean(grad, axis=0, keepdims=True)
    return inverse_std * (centred - unit * jnp.mean(grad * unit, axis=0, keepdims=True))


def low_pad(rows):
    return jnp.concatenate([rows, jnp.zeros_like(rows)], axis=0)


def high_pad(rows):
    return jnp.concatenate([jnp.zeros_like(rows), rows], axis=0)


def remote(src, dst, send_sem, recv_sem, device):
    return pltpu.make_async_remote_copy(
        src_ref=src,
        dst_ref=dst,
        send_sem=send_sem,
        recv_sem=recv_sem,
        device_id=device,
        device_id_type=pl.DeviceIdType.MESH,
    )


def kernel(
    sections, groups, tiles, micro, loss_scale,
    feat_any, labels_any, wup_any, wdown_any, head_any,
    both_out,
    feat, labels, wup, wdown, head, gathered, up_t, down_t, mix_t, up_n, down_n, head_pad, head_n,
    xbuf, obuf, nbuf, ubuf, istd, pre, hid, gpre, dybuf, dsend,
    parts, ry, rh, qbuf, rz, tbuf, rt, za, ysum, yall,
    in_sem, g_s, g_r, fs, fr, bs, br, rys, ryr, rhs_, rhr, rzs, rzr, ts, tr, zs, zr, ys, yr,
):
    s = lax.axis_index("section")
    f = lax.axis_index("fsdp")
    t = lax.axis_index("tile")
    y_low, z = f // RING, f % RING
    height = groups * tiles
    y = t * groups + y_low
    last = sections - 1
    block = 40 * RING
    hidden = block * groups
    fine = math.gcd(hidden, 128)

    def at(y_new, z_new):
        y_new = (y_new + 2 * height) % height
        z_new = (z_new + 2 * RING) % RING
        return {"fsdp": (y_new % groups) * RING + z_new, "tile": y_new // groups}

    copies_in = [
        pltpu.make_async_copy(source, target, in_sem.at[i])
        for i, (source, target) in enumerate(
            ((wup_any, wup), (wdown_any, wdown), (feat_any, feat), (labels_any, labels), (head_any, head))
        )
    ]
    for copy in copies_in:
        copy.start()

    barrier = pltpu.get_barrier_semaphore()
    partners = [at(y, z + d) for d in range(1, RING)]
    partners += [at(y + d, z) for d in range(1, height)]
    for device in partners:
        pl.semaphore_signal(barrier, inc=1, device_id=device, device_id_type=pl.DeviceIdType.MESH)

    @pl.when(s > 0)
    def _():
        pl.semaphore_signal(
            barrier, inc=1, device_id={"section": s - 1}, device_id_type=pl.DeviceIdType.MESH
        )

    @pl.when(s < last)
    def _():
        pl.semaphore_signal(
            barrier, inc=1, device_id={"section": s + 1}, device_id_type=pl.DeviceIdType.MESH
        )

    for copy in copies_in[:2]:
        copy.wait()
    up_w, down_w = wup[...], wdown[...]
    mixed = nt(up_w[:, 256:], place(0)) + nt(down_w[:, 256:], place(64))
    pieces = [up_w[:, :128], up_w[:, 128:256], down_w[:, :128], down_w[:, 128:256]]
    pieces = [piece.astype(f32) for piece in pieces] + [mixed, jnp.zeros((8, LANES), f32)]
    gathered[f] = jnp.concatenate(pieces, axis=0).astype(bf16)

    pl.semaphore_wait(
        barrier,
        len(partners) + jnp.where(s > 0, 1, 0) + jnp.where(s < last, 1, 0),
    )

    def slot(j, dz):
        return ((y_low + j) % groups) * RING + (z + dz + 2 * RING) % RING

    order = (0, 1, 3, 2) if groups == 4 else (0,)
    far = RING // 2
    low_rows, high_rows = pl.ds(0, HALF), pl.ds(HALF, PACK - HALF)
    is_a = s % 2 == FIRST
    sum_a = s % 2 == FIRST_SUM

    def arrived(index):
        remote(
            gathered.at[index], gathered.at[index], g_s.at[0], g_r.at[index, 0], at(y, z + 1)
        ).wait_recv()

    def halves_arrived(index):
        for i, rows in enumerate((low_rows, high_rows)):
            remote(
                gathered.at[index, rows], gathered.at[index, rows],
                g_s.at[0], g_r.at[index, i], at(y, z + 1),
            ).wait_recv()

    def y_sends(index, first):
        if groups != 4:
            return []
        copies = [
            remote(gathered.at[index], gathered.at[index], g_s.at[first], g_r.at[index, 0], at(y + 1, z)),
            remote(gathered.at[index], gathered.at[index], g_s.at[first + 1], g_r.at[index, 0], at(y - 1, z)),
            remote(
                gathered.at[index, low_rows], gathered.at[index, low_rows],
                g_s.at[first + 2], g_r.at[index, 0], at(y + 2, z),
            ),
            remote(
                gathered.at[index, high_rows], gathered.at[index, high_rows],
                g_s.at[first + 3], g_r.at[index, 1], at(y - 2, z),
            ),
        ]
        for copy in copies:
            copy.start()
        return copies

    @pl.when(is_a)
    def _():
        sent = y_sends(f, 0)

        def z_send(index, d):
            copy = remote(
                gathered.at[index], gathered.at[index],
                g_s.at[len(sent)], g_r.at[index, 0], at(y, z + d),
            )
            copy.start()
            sent.append(copy)

        def is_early(j):
            return j in order[: (len(order) + 1) // 2]

        def spread(j):
            for side in (1, -1):
                if far > 1 or is_early(j) == (side == 1):
                    z_send(slot(j, 0), side)

        def forward_from(j, distance):
            for side in (1, -1):
                index = slot(j, -side * distance)
                arrived(index)
                if distance + 1 < far or is_early(j) == (side == 1):
                    z_send(index, side)

        spread(0)
        for j in order[1:3]:
            arrived(slot(j, 0))
            spread(j)
        if far > 1:
            forward_from(0, 1)
        if len(order) > 3:
            halves_arrived(slot(2, 0))
            spread(2)
        if far > 1:
            for j in order[1:]:
                forward_from(j, 1)
        if far > 2:
            for distance in (2, 3):
                for j in (0,) + order[1:]:
                    forward_from(j, distance)
        for j in order:
            arrived(slot(j, far))
        for copy in sent:
            copy.wait_send()

    near_first = [d for i in range(1, far) for d in (i, -i)] + [far]

    @pl.when(jnp.logical_not(is_a))
    def _():
        sent = []

        def z_send(index, d, rows=None, half=0):
            ref = gathered.at[index] if rows is None else gathered.at[index, rows]
            copy = remote(ref, ref, g_s.at[len(sent)], g_r.at[index, half], at(y, z + d))
            copy.start()
            sent.append(copy)

        for d in near_first:
            if abs(d) <= 2:
                z_send(f, d)
        sent += y_sends(f, len(sent))
        for d in near_first:
            index = slot(0, d)
            if abs(d) == 4:
                halves_arrived(index)
            else:
                arrived(index)
            if abs(d) == 2 and far == 4:
                side = -d // 2
                z_send(index, side)
                z_send(index, 2 * side, low_rows if side == 1 else high_rows, 0 if side == 1 else 1)
            sent += y_sends(index, len(sent))
        if groups == 4:
            for d in [0] + near_first:
                arrived(slot(1, d))
                arrived(slot(3, d))
                halves_arrived(slot(2, d))
        for copy in sent:
            copy.wait_send()

    for copy in copies_in[2:]:
        copy.wait()

    def unpack(pair, carry):
        first = gathered[2 * pair].astype(f32)
        second = gathered[2 * pair + 1].astype(f32)
        rows = pl.ds(pl.multiple_of(pair * 80, 16), 80)

        def both(i):
            return jnp.concatenate(
                [first[40 * i : 40 * i + 40], second[40 * i : 40 * i + 40]], axis=0
            ).astype(bf16)

        up_t[rows, 0:128] = both(0)
        up_t[rows, 128:256] = both(1)
        down_t[rows, 0:128] = both(2)
        down_t[rows, 128:256] = both(3)
        mix_t[rows, :] = both(4)
        return carry

    lax.fori_loop(0, groups * RING // 2, unpack, 0)
    wide = eye(256)
    down_n[0:256, :] = nt(wide, down_t[...]).astype(bf16)
    turned = nt(eye(128), mix_t[...]).astype(bf16)
    down_n[256:320, :] = turned[64:128]

    @pl.when(s > 0)
    def _():
        up_n[0:256, :] = nt(wide, up_t[...]).astype(bf16)
        up_n[256:320, :] = turned[0:64]

    @pl.when(s == 0)
    def _():
        for m in range(micro):
            xbuf[m] = feat[m]

    @pl.when(s == last)
    def _():
        head_pad[...] = jnp.zeros_like(head_pad)
        head_pad[0:5, :] = head[...]
        head_n[...] = nt(eye(320), head_pad[...]).astype(bf16)

    def forward(m, carry):
        @pl.when(s > 0)
        def _():
            remote(obuf.at[m], xbuf.at[m], fs.at[m], fr.at[m], {"section": s}).wait_recv()

        x = xbuf[m]
        unit, inverse_std = normalize(x)
        normed = unit.astype(bf16)
        ubuf[m] = unit
        istd[m] = inverse_std
        nbuf[m] = normed
        low, high = normed[:256], low_pad(normed[256:])
        total = x.astype(f32)
        for first in range(0, hidden, fine):
            rows = slice(first, first + fine)
            before = nn(up_t[rows, :], low) + nn(mix_t[rows, :], high)
            pre[m, rows, :] = before
            bent = jnp.tanh(GELU_C * (before + GELU_A * (before * before * before)))
            hid[m, rows, :] = (before * (0.5 * (1.0 + bent))).astype(bf16)
        out = (total + nn(down_n[...], hid[m])).astype(bf16)
        obuf[m] = out

        @pl.when(s < last)
        def _():
            remote(obuf.at[m], xbuf.at[m], fs.at[m], fr.at[m], {"section": s + 1}).start()

        @pl.when(s == last)
        def _():
            head_unit, head_istd = normalize(obuf[m])
            logits = nn(head_pad[0:16, :], head_unit.astype(bf16))[0:8]
            classes = lax.broadcasted_iota(jnp.int32, logits.shape, 0)
            exponent = jnp.where(classes < 5, jnp.exp(logits), 0.0)
            probs = exponent / jnp.sum(exponent, axis=0, keepdims=True)
            onehot = jnp.where(classes == labels[pl.ds(m, 1), :], 1.0, 0.0)
            grad_logits = (probs - onehot) * loss_scale
            grad_logits = jnp.concatenate(
                [grad_logits, jnp.zeros((LANES - 8, LANES), f32)], axis=0
            ).astype(bf16)
            grad_norm = nn(head_n[...], grad_logits)
            dybuf[m] = norm_back(head_unit, head_istd, grad_norm).astype(bf16)

        return carry

    lax.fori_loop(0, micro, forward, 0)

    def backward(m, carry):
        @pl.when(s < last)
        def _():
            remote(dsend.at[m], dybuf.at[m], bs.at[m], br.at[m], {"section": s}).wait_recv()

        dy = dybuf[m]
        low, high = dy[:256], high_pad(dy[256:])
        for first in range(0, hidden, fine // 2):
            rows = slice(first, first + fine // 2)
            grad_hidden = nn(down_t[rows, :], low) + nn(mix_t[rows, :], high)
            before = pre[m, rows, :]
            square = before * before
            bent = jnp.tanh(before * (GELU_C + (GELU_C * GELU_A) * square))
            share = 0.5 + 0.5 * bent
            slope = share + (share * (1.0 - bent)) * (
                before * (GELU_C + (3.0 * GELU_C * GELU_A) * square)
            )
            gpre[m, rows, :] = (grad_hidden * slope).astype(bf16)

        @pl.when(s > 0)
        def _():
            grad_norm = nn(up_n[...], gpre[m])
            grad_in = dybuf[m].astype(f32) + norm_back(ubuf[m], istd[m], grad_norm)
            dsend[m] = grad_in.astype(bf16)
            remote(dsend.at[m], dybuf.at[m], bs.at[m], br.at[m], {"section": s - 1}).start()

        return carry

    lax.fori_loop(0, micro, backward, 0)

    normed = jnp.concatenate([nbuf[m] for m in range(micro)], axis=1)
    grads = jnp.concatenate([dybuf[m] for m in range(micro)], axis=1)
    normed_low, normed_high = normed[:256], low_pad(normed[256:])
    grads_low, grads_high = grads[:256], high_pad(grads[256:])

    def weight_grads(g):
        rows = pl.ds(pl.multiple_of(g * block, 16), block)
        grad_pre = jnp.concatenate([gpre[m, rows, :] for m in range(micro)], axis=1)
        active = jnp.concatenate([hid[m, rows, :] for m in range(micro)], axis=1)
        up = nt(grad_pre, normed_low)
        down = nt(active, grads_low)
        mix = nt(grad_pre, normed_high) + nt(active, grads_high)
        for k in range(RING):
            r = slice(40 * k, 40 * k + 40)
            parts[g, k] = jnp.concatenate(
                [up[r, :128], up[r, 128:], down[r, :128], down[r, 128:], mix[r],
                 jnp.zeros((8, LANES), f32)], axis=0,
            ).astype(bf16)

    def write(result):
        both_out[0:40, 0:128] = result[0:40]
        both_out[0:40, 128:256] = result[40:80]
        both_out[0:40, 256:320] = result[160:200, 0:64]
        both_out[40:80, 0:128] = result[80:120]
        both_out[40:80, 128:256] = result[120:160]
        both_out[40:80, 256:320] = result[160:200, 64:128]

    @pl.when(sum_a)
    def _():
        sent = []
        sides = tuple(enumerate((1, -1)))

        def is_early(where):
            return where < (groups + 1) // 2

        def pass_on(i, side, where, distance, level, hops, add=None):
            g = (y_low + where) % groups
            k = (z + side * distance + RING) % RING
            source = parts.at[g, k]
            if add is not None:
                source = za.at[i, add, where]
                remote(source, source, zs.at[0], zr.at[i, add, where], at(y, z + 1)).wait_recv()
                source[...] = (source[...].astype(f32) + parts[g, k].astype(f32)).astype(bf16)
            copy = remote(
                source, za.at[i, level, where],
                zs.at[len(sent)], zr.at[i, level, where], at(y, z + side * hops),
            )
            copy.start()
            sent.append(copy)

        for where in range(groups):
            weight_grads((y_low + where) % groups)
            if far == 4:
                for i, side in sides:
                    if is_early(where) == (side == 1):
                        pass_on(i, side, where, 4, 0, 1)
                    else:
                        pass_on(i, side, where, 3, 1, 1)
        for where in range(groups):
            for i, side in sides:
                if far == 4 or is_early(where) == (side == 1):
                    pass_on(i, side, where, 1, far - 1, 1)
        if far == 4:
            for where in range(groups):
                for i, side in sides:
                    if is_early(where) == (side == 1):
                        pass_on(i, side, where, 3, 1, 1, add=0)
            for late in (True, False):
                for where in range(groups):
                    for i, side in sides:
                        if (is_early(where) != (side == 1)) == late:
                            pass_on(i, side, where, 2, 2, 2, add=1)
        for where in ((0, 2, 1, 3) if groups == 4 else range(groups)):
            g = (y_low + where) % groups
            total = parts[g, z].astype(f32)
            for i, side in sides:
                for level in ((2, 3) if far == 4 else (0,)):
                    if far == 1 and is_early(where) != (side == 1):
                        continue
                    source = za.at[i, level, where]
                    remote(source, source, zs.at[0], zr.at[i, level, where], at(y, z + 1)).wait_recv()
                    total += source[...].astype(f32)
            ysum[where] = total.astype(bf16)
            for e in range(1, height):
                if e % groups == where:
                    copy = remote(ysum.at[where], yall.at[y], ys.at[e], yr.at[y], at(y + e, z))
                    copy.start()
                    sent.append(copy)
        yall[y] = ysum[0]
        for e in range(1, height):
            source = yall.at[(y + e) % height]
            remote(source, source, ys.at[0], yr.at[(y + e) % height], at(y, z + 1)).wait_recv()
        total = yall[0].astype(f32)
        for e in range(1, height):
            total += yall[e].astype(f32)
        write(total)
        for copy in sent:
            copy.wait_send()

    @pl.when(jnp.logical_not(sum_a))
    def _():
        sent = []
        far_first = [far] + [d for i in range(1, far) for d in (far - i, far + i)]
        if groups == 4:
            g = (y_low + 2) % groups
            weight_grads(g)
            for d in far_first + [0]:
                k = (z + d) % RING
                copy = remote(
                    parts.at[g, k], rh.at[k], rhs_.at[d], rhr.at[k],
                    at(y + jnp.where(k < far, -2, 2), z),
                )
                copy.start()
                sent.append(copy)
            for g in ((y_low + 1) % groups, (y_low + 3) % groups):
                weight_grads(g)
            for d in far_first + [0]:
                k = (z + d) % RING
                for i, side in enumerate((1, -1)):
                    g = (y_low + side + groups) % groups
                    copy = remote(parts.at[g, k], ry.at[i, k], rys.at[i, d], ryr.at[i, k], at(y + side, z))
                    copy.start()
                    sent.append(copy)
        weight_grads(y_low)

        def group_sum(k):
            total = parts[y_low, k].astype(f32)
            if groups == 4:
                remote(rh.at[k], rh.at[k], rhs_.at[0], rhr.at[k], at(y, z + 1)).wait_recv()
                for i in range(2):
                    remote(ry.at[i, k], ry.at[i, k], rys.at[i, 0], ryr.at[i, k], at(y, z + 1)).wait_recv()
                total += ry[0, k].astype(f32) + ry[1, k].astype(f32) + rh[k].astype(f32)
            return total

        for d in far_first:
            k = (z + d) % RING
            qbuf[k] = group_sum(k).astype(bf16)
            copy = remote(qbuf.at[k], rz.at[d - 1], rzs.at[d - 1], rzr.at[d - 1], at(y, z + d))
            copy.start()
            sent.append(copy)
        result = group_sum(z)
        for d in range(1, RING):
            remote(rz.at[d - 1], rz.at[d - 1], rzs.at[0], rzr.at[d - 1], at(y, z + 1)).wait_recv()
            result += rz[d - 1].astype(f32)
        if tiles == 2:
            rounded = result.astype(bf16)
            tbuf[...] = rounded
            copy = remote(tbuf, rt, ts.at[0], tr.at[0], at(y + groups, z))
            copy.start()
            sent.append(copy)
            copy.wait_recv()
            result = rounded.astype(f32) + rt[...].astype(f32)
        write(result)
        for copy in sent:
            copy.wait_send()

    @pl.when(s < last)
    def _():
        for m in range(micro):
            remote(obuf.at[m], xbuf.at[m], fs.at[m], fr.at[m], {"section": s + 1}).wait_send()

    @pl.when(s > 0)
    def _():
        for m in range(micro):
            remote(dsend.at[m], dybuf.at[m], bs.at[m], br.at[m], {"section": s - 1}).wait_send()


def local(features, labels, w_expand, w_reduce, head_weight):
    sections, shards, tiles = (lax.axis_size(a) for a in ("section", "fsdp", "tile"))
    groups = shards // RING
    micro, rows, width = features.shape
    hidden = 40 * shards
    loss_scale = 1.0 / math.sqrt(micro * rows * shards * tiles)
    vmem, dma = pltpu.VMEM, pltpu.SemaphoreType.DMA
    half = RING // 2

    def body(*refs):
        kernel(sections, groups, tiles, micro, loss_scale, *refs)

    both = pl.pallas_call(
        body,
        out_shape=jax.ShapeDtypeStruct((80, width), f32),
        in_specs=[pl.BlockSpec(memory_space=pl.ANY)] * 5,
        out_specs=pl.BlockSpec(memory_space=pltpu.VMEM),
        scratch_shapes=[
            vmem((micro, width, rows), bf16),
            vmem((micro, rows), jnp.int32),
            vmem((40, width), bf16),
            vmem((40, width), bf16),
            vmem((5, width), bf16),
            vmem((shards, PACK, LANES), bf16),
            vmem((hidden, 256), bf16),
            vmem((hidden, 256), bf16),
            vmem((hidden, LANES), bf16),
            vmem((width, hidden), bf16),
            vmem((width, hidden), bf16),
            vmem((LANES, width), bf16),
            vmem((width, LANES), bf16),
            vmem((micro, width, rows), bf16),
            vmem((micro, width, rows), bf16),
            vmem((micro, width, rows), bf16),
            vmem((micro, width, rows), f32),
            vmem((micro, 1, rows), f32),
            vmem((micro, hidden, rows), f32),
            vmem((micro, hidden, rows), bf16),
            vmem((micro, hidden, rows), bf16),
            vmem((micro, width, rows), bf16),
            vmem((micro, width, rows), bf16),
            vmem((groups, RING, PACK, LANES), bf16),
            vmem((2, RING, PACK, LANES), bf16),
            vmem((RING, PACK, LANES), bf16),
            vmem((RING, PACK, LANES), bf16),
            vmem((RING - 1, PACK, LANES), bf16),
            vmem((PACK, LANES), bf16),
            vmem((PACK, LANES), bf16),
            vmem((2, half, groups, PACK, LANES), bf16),
            vmem((groups, PACK, LANES), bf16),
            vmem((groups * tiles, PACK, LANES), bf16),
            dma((5,)),
            dma((7 * RING,)),
            dma((shards, 2)),
            dma((micro,)),
            dma((micro,)),
            dma((micro,)),
            dma((micro,)),
            dma((2, RING)),
            dma((2, RING)),
            dma((RING,)),
            dma((RING,)),
            dma((RING - 1,)),
            dma((RING - 1,)),
            dma((1,)),
            dma((1,)),
            dma((groups * RING,)),
            dma((2, half, groups)),
            dma((groups * tiles,)),
            dma((groups * tiles,)),
        ],
        compiler_params=pltpu.CompilerParams(
            collective_id=0, has_side_effects=True, vmem_limit_bytes=60 * 1024 * 1024
        ),
    )(features.transpose(0, 2, 1), labels, w_expand[0].T, w_reduce[0].T, head_weight.T)
    return both[:40].T[None], both[40:].T[None]


def solution(mesh):
    return jax.shard_map(
        local,
        mesh=mesh,
        in_specs=(
            P(None, ("fsdp", "tile"), None),
            P(None, ("fsdp", "tile")),
            P("section", None, "fsdp"),
            P("section", None, "fsdp"),
            P(),
        ),
        out_specs=(P("section", None, "fsdp"), P("section", None, "fsdp")),
        check_vma=False,
    )
```

```python
import math

import jax
import jax.numpy as jnp
from jax import lax
from jax.experimental import pallas as pl
from jax.experimental.pallas import tpu as pltpu
from jax.sharding import PartitionSpec as P

norm_eps = 1e-06
RING = 8
LANES = 128
PACK = 208
HALF = 112
FIRST = 1
FIRST_SUM = 1
GELU_C = math.sqrt(2.0 / math.pi)
GELU_A = 0.044715
bf16 = jnp.bfloat16
f32 = jnp.float32


def nt(lhs, rhs):
    return lax.dot_general(lhs, rhs, (((1,), (1,)), ((), ())), preferred_element_type=f32)


def nn(lhs, rhs):
    return jnp.dot(lhs, rhs, preferred_element_type=f32)


def eye(size):
    row = lax.broadcasted_iota(jnp.int32, (size, size), 0)
    column = lax.broadcasted_iota(jnp.int32, (size, size), 1)
    return jnp.where(row == column, 1.0, 0.0).astype(bf16)


def place(shift):
    row = lax.broadcasted_iota(jnp.int32, (LANES, 64), 0)
    column = lax.broadcasted_iota(jnp.int32, (LANES, 64), 1)
    return jnp.where(row == column + shift, 1.0, 0.0).astype(bf16)


def normalize(values):
    floats = values.astype(f32)
    centred = floats - jnp.mean(floats, axis=0, keepdims=True)
    inverse_std = lax.rsqrt(jnp.mean(centred * centred, axis=0, keepdims=True) + norm_eps)
    return centred * inverse_std, inverse_std


def norm_back(unit, inverse_std, grad):
    centred = grad - jnp.mean(grad, axis=0, keepdims=True)
    return inverse_std * (centred - unit * jnp.mean(grad * unit, axis=0, keepdims=True))


def low_pad(rows):
    return jnp.concatenate([rows, jnp.zeros_like(rows)], axis=0)


def high_pad(rows):
    return jnp.concatenate([jnp.zeros_like(rows), rows], axis=0)


def remote(src, dst, send_sem, recv_sem, device):
    return pltpu.make_async_remote_copy(
        src_ref=src,
        dst_ref=dst,
        send_sem=send_sem,
        recv_sem=recv_sem,
        device_id=device,
        device_id_type=pl.DeviceIdType.MESH,
    )


def kernel(
    sections, groups, tiles, micro, loss_scale,
    feat_any, labels_any, wup_any, wdown_any, head_any,
    both_out,
    feat, labels, wup, wdown, head, gathered, up_t, down_t, mix_t, up_n, down_n, head_pad, head_n,
    xbuf, obuf, nbuf, ubuf, istd, pre, hid, gpre, dybuf, dsend,
    parts, ry, rh, qbuf, rz, tbuf, rt, za, ysum, yall,
    in_sem, g_s, g_r, fs, fr, bs, br, rys, ryr, rhs_, rhr, rzs, rzr, ts, tr, zs, zr, ys, yr,
):
    s = lax.axis_index("section")
    f = lax.axis_index("fsdp")
    t = lax.axis_index("tile")
    y_low, z = f // RING, f % RING
    height = groups * tiles
    y = t * groups + y_low
    last = sections - 1
    block = 40 * RING
    hidden = block * groups
    fine = math.gcd(hidden, 128)

    def at(y_new, z_new):
        y_new = (y_new + 2 * height) % height
        z_new = (z_new + 2 * RING) % RING
        return {"fsdp": (y_new % groups) * RING + z_new, "tile": y_new // groups}

    copies_in = [
        pltpu.make_async_copy(source, target, in_sem.at[i])
        for i, (source, target) in enumerate(
            ((wup_any, wup), (wdown_any, wdown), (feat_any, feat), (labels_any, labels), (head_any, head))
        )
    ]
    for copy in copies_in:
        copy.start()

    barrier = pltpu.get_barrier_semaphore()
    def near(size):
        return (1, -1, 2, -2) if size > 4 else range(1, size)

    partners = [at(y, z + d) for d in near(RING)] + [at(y + d, z) for d in near(height)]
    for device in partners:
        pl.semaphore_signal(barrier, inc=1, device_id=device, device_id_type=pl.DeviceIdType.MESH)

    @pl.when(s > 0)
    def _():
        pl.semaphore_signal(
            barrier, inc=1, device_id={"section": s - 1}, device_id_type=pl.DeviceIdType.MESH
        )

    @pl.when(s < last)
    def _():
        pl.semaphore_signal(
            barrier, inc=1, device_id={"section": s + 1}, device_id_type=pl.DeviceIdType.MESH
        )

    for copy in copies_in[:2]:
        copy.wait()
    up_w, down_w = wup[...], wdown[...]
    mixed = nt(up_w[:, 256:], place(0)) + nt(down_w[:, 256:], place(64))
    pieces = [up_w[:, :128], up_w[:, 128:256], down_w[:, :128], down_w[:, 128:256]]
    pieces = [piece.astype(f32) for piece in pieces] + [mixed, jnp.zeros((8, LANES), f32)]
    gathered[f] = jnp.concatenate(pieces, axis=0).astype(bf16)

    pl.semaphore_wait(
        barrier,
        len(partners) + jnp.where(s > 0, 1, 0) + jnp.where(s < last, 1, 0),
    )

    def slot(j, dz):
        return ((y_low + j) % groups) * RING + (z + dz + 2 * RING) % RING

    order = (0, 1, 3, 2) if groups == 4 else (0,)
    far = RING // 2
    low_rows, high_rows = pl.ds(0, HALF), pl.ds(HALF, PACK - HALF)
    is_a = s % 2 == FIRST
    sum_a = s % 2 == FIRST_SUM

    def arrived(index):
        remote(
            gathered.at[index], gathered.at[index], g_s.at[0], g_r.at[index, 0], at(y, z + 1)
        ).wait_recv()

    def halves_arrived(index):
        for i, rows in enumerate((low_rows, high_rows)):
            remote(
                gathered.at[index, rows], gathered.at[index, rows],
                g_s.at[0], g_r.at[index, i], at(y, z + 1),
            ).wait_recv()

    def y_sends(index, first):
        if groups != 4:
            return []
        copies = [
            remote(gathered.at[index], gathered.at[index], g_s.at[first], g_r.at[index, 0], at(y + 1, z)),
            remote(gathered.at[index], gathered.at[index], g_s.at[first + 1], g_r.at[index, 0], at(y - 1, z)),
            remote(
                gathered.at[index, low_rows], gathered.at[index, low_rows],
                g_s.at[first + 2], g_r.at[index, 0], at(y + 2, z),
            ),
            remote(
                gathered.at[index, high_rows], gathered.at[index, high_rows],
                g_s.at[first + 3], g_r.at[index, 1], at(y - 2, z),
            ),
        ]
        for copy in copies:
            copy.start()
        return copies

    def unpack(pair, carry):
        first = gathered[2 * pair].astype(f32)
        second = gathered[2 * pair + 1].astype(f32)
        rows = pl.ds(pl.multiple_of(pair * 80, 16), 80)

        def both(i):
            return jnp.concatenate(
                [first[40 * i : 40 * i + 40], second[40 * i : 40 * i + 40]], axis=0
            ).astype(bf16)

        up_t[rows, 0:128] = both(0)
        up_t[rows, 128:256] = both(1)
        down_t[rows, 0:128] = both(2)
        down_t[rows, 128:256] = both(3)
        mix_t[rows, :] = both(4)
        return carry

    pairs = RING // 2
    soon, late = ((0, 1, 3), 2) if far == 4 else ((), 0)

    def unpack_column(r):
        def one(j, carry):
            return unpack((y_low + j) % groups * pairs + (z // 2 + r) % pairs, carry)

        lax.fori_loop(0, groups, one, 0)

    @pl.when(is_a)
    def _():
        sent = y_sends(f, 0)

        def z_send(index, d):
            copy = remote(
                gathered.at[index], gathered.at[index],
                g_s.at[len(sent)], g_r.at[index, 0], at(y, z + d),
            )
            copy.start()
            sent.append(copy)

        def is_early(j):
            return j in order[: (len(order) + 1) // 2]

        def spread(j):
            for side in (1, -1):
                if far > 1 or is_early(j) == (side == 1):
                    z_send(slot(j, 0), side)

        def forward_from(j, distance):
            for side in (1, -1):
                index = slot(j, -side * distance)
                arrived(index)
                if distance + 1 < far or is_early(j) == (side == 1):
                    z_send(index, side)

        spread(0)
        for j in order[1:3]:
            arrived(slot(j, 0))
            spread(j)
        if far > 1:
            forward_from(0, 1)
        if len(order) > 3:
            halves_arrived(slot(2, 0))
            spread(2)
        if far > 1:
            for j in order[1:]:
                forward_from(j, 1)
        if far > 2:
            for distance in (2, 3):
                for j in (0,) + order[1:]:
                    forward_from(j, distance)
        for r in soon:
            unpack_column(r)
        for j in order:
            arrived(slot(j, far))
        unpack_column(late)
        for copy in sent:
            copy.wait_send()

    near_first = [d for i in range(1, far) for d in (i, -i)] + [far]

    @pl.when(jnp.logical_not(is_a))
    def _():
        sent = []

        def z_send(index, d, rows=None, half=0):
            ref = gathered.at[index] if rows is None else gathered.at[index, rows]
            copy = remote(ref, ref, g_s.at[len(sent)], g_r.at[index, half], at(y, z + d))
            copy.start()
            sent.append(copy)

        for d in (2, -2, 1, -1) if far == 4 else near_first:
            z_send(f, d)
        sent += y_sends(f, len(sent))
        if far == 4:
            for side in (1, -1):
                index = slot(0, -2 * side)
                arrived(index)
                z_send(index, side)
                z_send(index, 2 * side, low_rows if side == 1 else high_rows, 0 if side == 1 else 1)
        for d in near_first:
            index = slot(0, d)
            if abs(d) == 4:
                halves_arrived(index)
            elif abs(d) != 2:
                arrived(index)
            sent += y_sends(index, len(sent))
        for r in soon + (late,):
            if groups == 4:
                first = (z // 2 + r) % pairs * 2
                for j in (1, 3, 2):
                    for index in (first, first + 1):
                        index += (y_low + j) % groups * RING
                        (halves_arrived if j == 2 else arrived)(index)
            unpack_column(r)
        for copy in sent:
            copy.wait_send()

    for copy in copies_in[2:]:
        copy.wait()

    wide = eye(256)
    down_n[0:256, :] = nt(wide, down_t[...]).astype(bf16)
    turned = nt(eye(128), mix_t[...]).astype(bf16)
    down_n[256:320, :] = turned[64:128]

    @pl.when(s > 0)
    def _():
        up_n[0:256, :] = nt(wide, up_t[...]).astype(bf16)
        up_n[256:320, :] = turned[0:64]

    @pl.when(s == 0)
    def _():
        for m in range(micro):
            xbuf[m] = feat[m]

    @pl.when(s == last)
    def _():
        head_pad[...] = jnp.zeros_like(head_pad)
        head_pad[0:5, :] = head[...]
        head_n[...] = nt(eye(320), head_pad[...]).astype(bf16)

    def forward(m, carry):
        @pl.when(s > 0)
        def _():
            remote(obuf.at[m], xbuf.at[m], fs.at[m], fr.at[m], {"section": s}).wait_recv()

        x = xbuf[m]
        unit, inverse_std = normalize(x)
        normed = unit.astype(bf16)
        ubuf[m] = unit
        istd[m] = inverse_std
        nbuf[m] = normed
        low, high = normed[:256], low_pad(normed[256:])
        total = x.astype(f32)
        for first in range(0, hidden, fine):
            rows = slice(first, first + fine)
            before = nn(up_t[rows, :], low) + nn(mix_t[rows, :], high)
            pre[m, rows, :] = before
            bent = jnp.tanh(GELU_C * (before + GELU_A * (before * before * before)))
            hid[m, rows, :] = (before * (0.5 * (1.0 + bent))).astype(bf16)
        out = (total + nn(down_n[...], hid[m])).astype(bf16)
        obuf[m] = out

        @pl.when(s < last)
        def _():
            remote(obuf.at[m], xbuf.at[m], fs.at[m], fr.at[m], {"section": s + 1}).start()

        return carry

    lax.fori_loop(0, micro, forward, 0)

    @pl.when(s == last)
    def _():
        for m in range(micro):
            head_unit, head_istd = normalize(obuf[m])
            logits = nn(head_pad[0:16, :], head_unit.astype(bf16))[0:8]
            classes = lax.broadcasted_iota(jnp.int32, logits.shape, 0)
            exponent = jnp.where(classes < 5, jnp.exp(logits), 0.0)
            probs = exponent / jnp.sum(exponent, axis=0, keepdims=True)
            onehot = jnp.where(classes == labels[m : m + 1, :], 1.0, 0.0)
            grad_logits = (probs - onehot) * loss_scale
            grad_logits = jnp.concatenate(
                [grad_logits, jnp.zeros((LANES - 8, LANES), f32)], axis=0
            ).astype(bf16)
            grad_norm = nn(head_n[...], grad_logits)
            dybuf[m] = norm_back(head_unit, head_istd, grad_norm).astype(bf16)

    def backward(m, carry):
        @pl.when(s < last)
        def _():
            remote(dsend.at[m], dybuf.at[m], bs.at[m], br.at[m], {"section": s}).wait_recv()

        dy = dybuf[m]
        low, high = dy[:256], high_pad(dy[256:])
        for first in range(0, hidden, fine // 2):
            rows = slice(first, first + fine // 2)
            grad_hidden = nn(down_t[rows, :], low) + nn(mix_t[rows, :], high)
            before = pre[m, rows, :]
            square = before * before
            bent = jnp.tanh(before * (GELU_C + (GELU_C * GELU_A) * square))
            share = 0.5 + 0.5 * bent
            slope = share + (share * (1.0 - bent)) * (
                before * (GELU_C + (3.0 * GELU_C * GELU_A) * square)
            )
            gpre[m, rows, :] = (grad_hidden * slope).astype(bf16)

        @pl.when(s > 0)
        def _():
            grad_norm = nn(up_n[...], gpre[m])
            grad_in = dybuf[m].astype(f32) + norm_back(ubuf[m], istd[m], grad_norm)
            dsend[m] = grad_in.astype(bf16)
            remote(dsend.at[m], dybuf.at[m], bs.at[m], br.at[m], {"section": s - 1}).start()

        return carry

    lax.fori_loop(0, micro, backward, 0)

    normed = jnp.concatenate([nbuf[m] for m in range(micro)], axis=1)
    grads = jnp.concatenate([dybuf[m] for m in range(micro)], axis=1)
    normed_low, normed_high = normed[:256], low_pad(normed[256:])
    grads_low, grads_high = grads[:256], high_pad(grads[256:])

    def weight_grads(g):
        rows = pl.ds(pl.multiple_of(g * block, 16), block)
        grad_pre = jnp.concatenate([gpre[m, rows, :] for m in range(micro)], axis=1)
        active = jnp.concatenate([hid[m, rows, :] for m in range(micro)], axis=1)
        up = nt(grad_pre, normed_low)
        down = nt(active, grads_low)
        mix = nt(grad_pre, normed_high) + nt(active, grads_high)
        for k in range(RING):
            r = slice(40 * k, 40 * k + 40)
            parts[g, k] = jnp.concatenate(
                [up[r, :128], up[r, 128:], down[r, :128], down[r, 128:], mix[r],
                 jnp.zeros((8, LANES), f32)], axis=0,
            ).astype(bf16)

    def write(result):
        both_out[0:40, 0:128] = result[0:40]
        both_out[0:40, 128:256] = result[40:80]
        both_out[0:40, 256:320] = result[160:200, 0:64]
        both_out[40:80, 0:128] = result[80:120]
        both_out[40:80, 128:256] = result[120:160]
        both_out[40:80, 256:320] = result[160:200, 64:128]

    @pl.when(sum_a)
    def _():
        sent = []
        sides = tuple(enumerate((1, -1)))

        def is_early(where):
            return where < (groups + 1) // 2

        def pass_on(i, side, where, distance, level, hops, add=None):
            g = (y_low + where) % groups
            k = (z + side * distance + RING) % RING
            source = parts.at[g, k]
            if add is not None:
                source = za.at[i, add, where]
                remote(source, source, zs.at[0], zr.at[i, add, where], at(y, z + 1)).wait_recv()
                source[...] = (source[...].astype(f32) + parts[g, k].astype(f32)).astype(bf16)
            copy = remote(
                source, za.at[i, level, where],
                zs.at[len(sent)], zr.at[i, level, where], at(y, z + side * hops),
            )
            copy.start()
            sent.append(copy)

        for where in range(groups):
            weight_grads((y_low + where) % groups)
            if far == 4:
                for i, side in sides:
                    if is_early(where) == (side == 1):
                        pass_on(i, side, where, 4, 0, 1)
                    else:
                        pass_on(i, side, where, 3, 1, 1)
        for where in range(groups):
            for i, side in sides:
                if far == 4 or is_early(where) == (side == 1):
                    pass_on(i, side, where, 1, far - 1, 1)
        if far == 4:
            for where in range(groups):
                for i, side in sides:
                    if is_early(where) == (side == 1):
                        pass_on(i, side, where, 3, 1, 1, add=0)
            for late in (True, False):
                for where in range(groups):
                    for i, side in sides:
                        if (is_early(where) != (side == 1)) == late:
                            pass_on(i, side, where, 2, 2, 2, add=1)
        for where in ((0, 2, 1, 3) if groups == 4 else range(groups)):
            g = (y_low + where) % groups
            total = parts[g, z].astype(f32)
            for i, side in sides:
                for level in ((2, 3) if far == 4 else (0,)):
                    if far == 1 and is_early(where) != (side == 1):
                        continue
                    source = za.at[i, level, where]
                    remote(source, source, zs.at[0], zr.at[i, level, where], at(y, z + 1)).wait_recv()
                    total += source[...].astype(f32)
            ysum[where] = total.astype(bf16)
            for e in range(1, height):
                if e % groups == where:
                    copy = remote(ysum.at[where], yall.at[y], ys.at[e], yr.at[y], at(y + e, z))
                    copy.start()
                    sent.append(copy)
        yall[y] = ysum[0]
        for e in range(1, height):
            source = yall.at[(y + e) % height]
            remote(source, source, ys.at[0], yr.at[(y + e) % height], at(y, z + 1)).wait_recv()
        total = yall[0].astype(f32)
        for e in range(1, height):
            total += yall[e].astype(f32)
        write(total)
        for copy in sent:
            copy.wait_send()

    @pl.when(jnp.logical_not(sum_a))
    def _():
        sent = []
        far_first = [far] + [d for i in range(1, far) for d in (far - i, far + i)]
        if groups == 4:
            two = (y_low + 2) % groups
            weight_grads(two)
            for d in far_first + [0]:
                k = (z + d) % RING
                copy = remote(
                    parts.at[two, k], rh.at[k], rhs_.at[d], rhr.at[k],
                    at(y + jnp.where(k < far, -1, 1), z),
                )
                copy.start()
                sent.append(copy)
            for g in ((y_low + 1) % groups, (y_low + 3) % groups):
                weight_grads(g)

            def to_owner(d, relayed):
                k = (z + d) % RING
                side = jnp.where(k < far, 1, -1) * (-1 if relayed else 1)
                i = (1 - side) // 2
                g = (y_low + side + groups) % groups
                if relayed:
                    remote(rh.at[k], rh.at[k], rhs_.at[0], rhr.at[k], at(y, z + 1)).wait_recv()
                    parts[g, k] = (parts[g, k].astype(f32) + rh[k].astype(f32)).astype(bf16)
                copy = remote(
                    parts.at[g, k], ry.at[i, k], rys.at[1 if relayed else 0, d], ryr.at[i, k],
                    at(y + side, z),
                )
                copy.start()
                sent.append(copy)

            slots = far_first + [0]
            for d in slots[:far]:
                to_owner(d, False)
        weight_grads(y_low)
        if groups == 4:
            for i, d in enumerate(slots):
                to_owner(d, True)
                for later in slots[far + i : far + i + 1]:
                    to_owner(later, False)

        def group_sum(k):
            total = parts[y_low, k].astype(f32)
            if groups == 4:
                for i in range(2):
                    remote(ry.at[i, k], ry.at[i, k], rys.at[i, 0], ryr.at[i, k], at(y, z + 1)).wait_recv()
                total += ry[0, k].astype(f32) + ry[1, k].astype(f32)
            return total

        for d in far_first:
            k = (z + d) % RING
            qbuf[k] = group_sum(k).astype(bf16)
            copy = remote(qbuf.at[k], rz.at[d - 1], rzs.at[d - 1], rzr.at[d - 1], at(y, z + d))
            copy.start()
            sent.append(copy)
        result = group_sum(z)
        for d in range(1, RING):
            remote(rz.at[d - 1], rz.at[d - 1], rzs.at[0], rzr.at[d - 1], at(y, z + 1)).wait_recv()
            result += rz[d - 1].astype(f32)
        if tiles == 2:
            rounded = result.astype(bf16)
            tbuf[...] = rounded
            copy = remote(tbuf, rt, ts.at[0], tr.at[0], at(y + groups, z))
            copy.start()
            sent.append(copy)
            copy.wait_recv()
            result = rounded.astype(f32) + rt[...].astype(f32)
        write(result)
        for copy in sent:
            copy.wait_send()

    @pl.when(s < last)
    def _():
        for m in range(micro):
            remote(obuf.at[m], xbuf.at[m], fs.at[m], fr.at[m], {"section": s + 1}).wait_send()

    @pl.when(s > 0)
    def _():
        for m in range(micro):
            remote(dsend.at[m], dybuf.at[m], bs.at[m], br.at[m], {"section": s - 1}).wait_send()


def local(features, labels, w_expand, w_reduce, head_weight):
    sections, shards, tiles = (lax.axis_size(a) for a in ("section", "fsdp", "tile"))
    groups = shards // RING
    micro, rows, width = features.shape
    hidden = 40 * shards
    loss_scale = 1.0 / math.sqrt(micro * rows * shards * tiles)
    vmem, dma = pltpu.VMEM, pltpu.SemaphoreType.DMA
    half = RING // 2

    def body(*refs):
        kernel(sections, groups, tiles, micro, loss_scale, *refs)

    both = pl.pallas_call(
        body,
        out_shape=jax.ShapeDtypeStruct((80, width), f32),
        in_specs=[pl.BlockSpec(memory_space=pl.ANY)] * 5,
        out_specs=pl.BlockSpec(memory_space=pltpu.VMEM),
        scratch_shapes=[
            vmem((micro, width, rows), bf16),
            vmem((micro, rows), jnp.int32),
            vmem((40, width), bf16),
            vmem((40, width), bf16),
            vmem((5, width), bf16),
            vmem((shards, PACK, LANES), bf16),
            vmem((hidden, 256), bf16),
            vmem((hidden, 256), bf16),
            vmem((hidden, LANES), bf16),
            vmem((width, hidden), bf16),
            vmem((width, hidden), bf16),
            vmem((LANES, width), bf16),
            vmem((width, LANES), bf16),
            vmem((micro, width, rows), bf16),
            vmem((micro, width, rows), bf16),
            vmem((micro, width, rows), bf16),
            vmem((micro, width, rows), f32),
            vmem((micro, 1, rows), f32),
            vmem((micro, hidden, rows), f32),
            vmem((micro, hidden, rows), bf16),
            vmem((micro, hidden, rows), bf16),
            vmem((micro, width, rows), bf16),
            vmem((micro, width, rows), bf16),
            vmem((groups, RING, PACK, LANES), bf16),
            vmem((2, RING, PACK, LANES), bf16),
            vmem((RING, PACK, LANES), bf16),
            vmem((RING, PACK, LANES), bf16),
            vmem((RING - 1, PACK, LANES), bf16),
            vmem((PACK, LANES), bf16),
            vmem((PACK, LANES), bf16),
            vmem((2, half, groups, PACK, LANES), bf16),
            vmem((groups, PACK, LANES), bf16),
            vmem((groups * tiles, PACK, LANES), bf16),
            dma((5,)),
            dma((7 * RING,)),
            dma((shards, 2)),
            dma((micro,)),
            dma((micro,)),
            dma((micro,)),
            dma((micro,)),
            dma((2, RING)),
            dma((2, RING)),
            dma((RING,)),
            dma((RING,)),
            dma((RING - 1,)),
            dma((RING - 1,)),
            dma((1,)),
            dma((1,)),
            dma((groups * RING,)),
            dma((2, half, groups)),
            dma((groups * tiles,)),
            dma((groups * tiles,)),
        ],
        compiler_params=pltpu.CompilerParams(
            collective_id=0, has_side_effects=True, vmem_limit_bytes=60 * 1024 * 1024
        ),
    )(features.transpose(0, 2, 1), labels, w_expand[0].T, w_reduce[0].T, head_weight.T)
    return both[:40].T[None], both[40:].T[None]


def solution(mesh):
    return jax.shard_map(
        local,
        mesh=mesh,
        in_specs=(
            P(None, ("fsdp", "tile"), None),
            P(None, ("fsdp", "tile")),
            P("section", None, "fsdp"),
            P("section", None, "fsdp"),
            P(),
        ),
        out_specs=(P("section", None, "fsdp"), P("section", None, "fsdp")),
        check_vma=False,
    )
```

```python
import math

import jax
import jax.numpy as jnp
from jax import lax
from jax.experimental import pallas as pl
from jax.experimental.pallas import tpu as pltpu
from jax.sharding import PartitionSpec as P

norm_eps = 1e-06
RING = 8
LANES = 128
PACK = 208
HALF = 112
FIRST = 1
FIRST_SUM = 1
GELU_C = math.sqrt(2.0 / math.pi)
GELU_A = 0.044715
bf16 = jnp.bfloat16
f32 = jnp.float32


def nt(lhs, rhs):
    return lax.dot_general(lhs, rhs, (((1,), (1,)), ((), ())), preferred_element_type=f32)


def nn(lhs, rhs):
    return jnp.dot(lhs, rhs, preferred_element_type=f32)


def eye(size):
    row = lax.broadcasted_iota(jnp.int32, (size, size), 0)
    column = lax.broadcasted_iota(jnp.int32, (size, size), 1)
    return jnp.where(row == column, 1.0, 0.0).astype(bf16)


def place(shift):
    row = lax.broadcasted_iota(jnp.int32, (LANES, 64), 0)
    column = lax.broadcasted_iota(jnp.int32, (LANES, 64), 1)
    return jnp.where(row == column + shift, 1.0, 0.0).astype(bf16)


def normalize(values):
    floats = values.astype(f32)
    centred = floats - jnp.mean(floats, axis=0, keepdims=True)
    inverse_std = lax.rsqrt(jnp.mean(centred * centred, axis=0, keepdims=True) + norm_eps)
    return centred * inverse_std, inverse_std


def norm_back(unit, inverse_std, grad):
    centred = grad - jnp.mean(grad, axis=0, keepdims=True)
    return inverse_std * (centred - unit * jnp.mean(grad * unit, axis=0, keepdims=True))


def low_pad(rows):
    return jnp.concatenate([rows, jnp.zeros_like(rows)], axis=0)


def high_pad(rows):
    return jnp.concatenate([jnp.zeros_like(rows), rows], axis=0)


def remote(src, dst, send_sem, recv_sem, device):
    return pltpu.make_async_remote_copy(
        src_ref=src,
        dst_ref=dst,
        send_sem=send_sem,
        recv_sem=recv_sem,
        device_id=device,
        device_id_type=pl.DeviceIdType.MESH,
    )


def kernel(
    sections, groups, tiles, micro, loss_scale,
    feat_any, labels_any, wup_any, wdown_any, head_any,
    both_out,
    feat, labels, wup, wdown, head, gathered, up_t, down_t, mix_t, up_n, down_n, head_pad, head_n,
    xbuf, obuf, nbuf, ubuf, istd, pre, hid, gpre, dybuf, dsend,
    parts, ry, rh, qbuf, rz, tbuf, rt, za, ysum, yall,
    in_sem, g_s, g_r, fs, fr, bs, br, rys, ryr, rhs_, rhr, rzs, rzr, ts, tr, zs, zr, ys, yr,
):
    s = lax.axis_index("section")
    f = lax.axis_index("fsdp")
    t = lax.axis_index("tile")
    y_low, z = f // RING, f % RING
    height = groups * tiles
    y = t * groups + y_low
    last = sections - 1
    block = 40 * RING
    hidden = block * groups
    fine = math.gcd(hidden, 128)

    def at(y_new, z_new):
        y_new = (y_new + 2 * height) % height
        z_new = (z_new + 2 * RING) % RING
        return {"fsdp": (y_new % groups) * RING + z_new, "tile": y_new // groups}

    copies_in = [
        pltpu.make_async_copy(source, target, in_sem.at[i])
        for i, (source, target) in enumerate(
            ((wup_any, wup), (wdown_any, wdown), (feat_any, feat), (labels_any, labels), (head_any, head))
        )
    ]
    for copy in copies_in:
        copy.start()

    barrier = pltpu.get_barrier_semaphore()
    def near(size):
        return (1, -1, 2, -2) if size > 4 else range(1, size)

    partners = [at(y, z + d) for d in near(RING)] + [at(y + d, z) for d in near(height)]
    for device in partners:
        pl.semaphore_signal(barrier, inc=1, device_id=device, device_id_type=pl.DeviceIdType.MESH)

    @pl.when(s > 0)
    def _():
        pl.semaphore_signal(
            barrier, inc=1, device_id={"section": s - 1}, device_id_type=pl.DeviceIdType.MESH
        )

    @pl.when(s < last)
    def _():
        pl.semaphore_signal(
            barrier, inc=1, device_id={"section": s + 1}, device_id_type=pl.DeviceIdType.MESH
        )

    for copy in copies_in[:2]:
        copy.wait()
    up_w, down_w = wup[...], wdown[...]
    mixed = nt(up_w[:, 256:], place(0)) + nt(down_w[:, 256:], place(64))
    pieces = [up_w[:, :128], up_w[:, 128:256], down_w[:, :128], down_w[:, 128:256]]
    pieces = [piece.astype(f32) for piece in pieces] + [mixed, jnp.zeros((8, LANES), f32)]
    gathered[f] = jnp.concatenate(pieces, axis=0).astype(bf16)

    pl.semaphore_wait(
        barrier,
        len(partners) + jnp.where(s > 0, 1, 0) + jnp.where(s < last, 1, 0),
    )

    def slot(j, dz):
        return ((y_low + j) % groups) * RING + (z + dz + 2 * RING) % RING

    order = (0, 1, 3, 2) if groups == 4 else (0,)
    far = RING // 2
    low_rows, high_rows = pl.ds(0, HALF), pl.ds(HALF, PACK - HALF)
    is_a = s % 2 == FIRST
    sum_a = s % 2 == FIRST_SUM

    def arrived(index):
        remote(
            gathered.at[index], gathered.at[index], g_s.at[0], g_r.at[index, 0], at(y, z + 1)
        ).wait_recv()

    def halves_arrived(index):
        for i, rows in enumerate((low_rows, high_rows)):
            remote(
                gathered.at[index, rows], gathered.at[index, rows],
                g_s.at[0], g_r.at[index, i], at(y, z + 1),
            ).wait_recv()

    def y_sends(index, first):
        if groups != 4:
            return []
        copies = [
            remote(gathered.at[index], gathered.at[index], g_s.at[first], g_r.at[index, 0], at(y + 1, z)),
            remote(gathered.at[index], gathered.at[index], g_s.at[first + 1], g_r.at[index, 0], at(y - 1, z)),
            remote(
                gathered.at[index, low_rows], gathered.at[index, low_rows],
                g_s.at[first + 2], g_r.at[index, 0], at(y + 2, z),
            ),
            remote(
                gathered.at[index, high_rows], gathered.at[index, high_rows],
                g_s.at[first + 3], g_r.at[index, 1], at(y - 2, z),
            ),
        ]
        for copy in copies:
            copy.start()
        return copies

    def unpack(pair, carry):
        first = gathered[2 * pair].astype(f32)
        second = gathered[2 * pair + 1].astype(f32)
        rows = pl.ds(pl.multiple_of(pair * 80, 16), 80)

        def both(i):
            return jnp.concatenate(
                [first[40 * i : 40 * i + 40], second[40 * i : 40 * i + 40]], axis=0
            ).astype(bf16)

        up_t[rows, 0:128] = both(0)
        up_t[rows, 128:256] = both(1)
        down_t[rows, 0:128] = both(2)
        down_t[rows, 128:256] = both(3)
        mix_t[rows, :] = both(4)
        return carry

    pairs = RING // 2
    soon, late = ((0, 1, 3), 2) if far == 4 else ((), 0)

    def unpack_column(r):
        def one(j, carry):
            return unpack((y_low + j) % groups * pairs + (z // 2 + r) % pairs, carry)

        lax.fori_loop(0, groups, one, 0)

    @pl.when(is_a)
    def _():
        sent = y_sends(f, 0)

        def z_send(index, d):
            copy = remote(
                gathered.at[index], gathered.at[index],
                g_s.at[len(sent)], g_r.at[index, 0], at(y, z + d),
            )
            copy.start()
            sent.append(copy)

        def is_early(j):
            return j in order[: (len(order) + 1) // 2]

        def spread(j):
            for side in (1, -1):
                if far > 1 or is_early(j) == (side == 1):
                    z_send(slot(j, 0), side)

        def forward_from(j, distance):
            for side in (1, -1):
                index = slot(j, -side * distance)
                arrived(index)
                if distance + 1 < far or is_early(j) == (side == 1):
                    z_send(index, side)

        spread(0)
        for j in order[1:3]:
            arrived(slot(j, 0))
            spread(j)
        if far > 1:
            forward_from(0, 1)
        if len(order) > 3:
            halves_arrived(slot(2, 0))
            spread(2)
        if far > 1:
            for j in order[1:]:
                forward_from(j, 1)
        if far > 2:
            for distance in (2, 3):
                for j in (0,) + order[1:]:
                    forward_from(j, distance)
        for r in soon:
            unpack_column(r)
        for copy in sent:
            copy.wait_send()
        for j in order:
            arrived(slot(j, far))
        unpack_column(late)

    near_first = [d for i in range(1, far) for d in (i, -i)] + [far]

    @pl.when(jnp.logical_not(is_a))
    def _():
        sent = []

        def z_send(index, d, rows=None, half=0):
            ref = gathered.at[index] if rows is None else gathered.at[index, rows]
            copy = remote(ref, ref, g_s.at[len(sent)], g_r.at[index, half], at(y, z + d))
            copy.start()
            sent.append(copy)

        for d in (2, -2, 1, -1) if far == 4 else near_first:
            z_send(f, d)
        sent += y_sends(f, len(sent))
        if far == 4:
            for side in (1, -1):
                index = slot(0, -2 * side)
                arrived(index)
                z_send(index, side)
                z_send(index, 2 * side, low_rows if side == 1 else high_rows, 0 if side == 1 else 1)
        for d in near_first:
            index = slot(0, d)
            if abs(d) == 4:
                halves_arrived(index)
            elif abs(d) != 2:
                arrived(index)
            sent += y_sends(index, len(sent))
        for r in soon + (late,):
            if r == late:
                for copy in sent:
                    copy.wait_send()
            if groups == 4:
                first = (z // 2 + r) % pairs * 2
                for j in (1, 3, 2):
                    for index in (first, first + 1):
                        index += (y_low + j) % groups * RING
                        (halves_arrived if j == 2 else arrived)(index)
            unpack_column(r)

    for copy in copies_in[2:]:
        copy.wait()

    wide = eye(256)
    down_n[0:256, :] = nt(wide, down_t[...]).astype(bf16)
    turned = nt(eye(128), mix_t[...]).astype(bf16)
    down_n[256:320, :] = turned[64:128]

    @pl.when(s > 0)
    def _():
        up_n[0:256, :] = nt(wide, up_t[...]).astype(bf16)
        up_n[256:320, :] = turned[0:64]

    @pl.when(s == 0)
    def _():
        for m in range(micro):
            xbuf[m] = feat[m]

    @pl.when(s == last)
    def _():
        head_pad[...] = jnp.zeros_like(head_pad)
        head_pad[0:5, :] = head[...]
        head_n[...] = nt(eye(320), head_pad[...]).astype(bf16)

    def forward(m, carry):
        @pl.when(s > 0)
        def _():
            remote(obuf.at[m], xbuf.at[m], fs.at[m], fr.at[m], {"section": s}).wait_recv()

        x = xbuf[m]
        unit, inverse_std = normalize(x)
        normed = unit.astype(bf16)
        ubuf[m] = unit
        istd[m] = inverse_std
        nbuf[m] = normed
        low, high = normed[:256], low_pad(normed[256:])
        total = x.astype(f32)
        active = []
        for first in range(0, hidden, fine):
            rows = slice(first, first + fine)
            before = nn(up_t[rows, :], low) + nn(mix_t[rows, :], high)
            pre[m, rows, :] = before
            bent = jnp.tanh(GELU_C * (before + GELU_A * (before * before * before)))
            active.append((before * (0.5 * (1.0 + bent))).astype(bf16))
            hid[m, rows, :] = active[-1]
        out = (total + nn(down_n[...], jnp.concatenate(active, axis=0))).astype(bf16)
        obuf[m] = out

        @pl.when(s < last)
        def _():
            remote(obuf.at[m], xbuf.at[m], fs.at[m], fr.at[m], {"section": s + 1}).start()

        return carry

    lax.fori_loop(0, micro, forward, 0)

    @pl.when(s == last)
    def _():
        for m in range(micro):
            head_unit, head_istd = normalize(obuf[m])
            logits = nn(head_pad[0:16, :], head_unit.astype(bf16))[0:8]
            classes = lax.broadcasted_iota(jnp.int32, logits.shape, 0)
            exponent = jnp.where(classes < 5, jnp.exp(logits), 0.0)
            probs = exponent / jnp.sum(exponent, axis=0, keepdims=True)
            onehot = jnp.where(classes == labels[m : m + 1, :], 1.0, 0.0)
            grad_logits = (probs - onehot) * loss_scale
            grad_logits = jnp.concatenate(
                [grad_logits, jnp.zeros((LANES - 8, LANES), f32)], axis=0
            ).astype(bf16)
            grad_norm = nn(head_n[...], grad_logits)
            dybuf[m] = norm_back(head_unit, head_istd, grad_norm).astype(bf16)

    def backward(m, carry):
        @pl.when(s < last)
        def _():
            remote(dsend.at[m], dybuf.at[m], bs.at[m], br.at[m], {"section": s}).wait_recv()

        dy = dybuf[m]
        low, high = dy[:256], high_pad(dy[256:])
        for first in range(0, hidden, fine // 2):
            rows = slice(first, first + fine // 2)
            grad_hidden = nn(down_t[rows, :], low) + nn(mix_t[rows, :], high)
            before = pre[m, rows, :]
            square = before * before
            bent = jnp.tanh(before * (GELU_C + (GELU_C * GELU_A) * square))
            share = 0.5 + 0.5 * bent
            slope = share + (share * (1.0 - bent)) * (
                before * (GELU_C + (3.0 * GELU_C * GELU_A) * square)
            )
            gpre[m, rows, :] = (grad_hidden * slope).astype(bf16)

        @pl.when(s > 0)
        def _():
            grad_norm = nn(up_n[...], gpre[m])
            grad_in = dybuf[m].astype(f32) + norm_back(ubuf[m], istd[m], grad_norm)
            dsend[m] = grad_in.astype(bf16)
            remote(dsend.at[m], dybuf.at[m], bs.at[m], br.at[m], {"section": s - 1}).start()

        return carry

    lax.fori_loop(0, micro, backward, 0)

    normed = jnp.concatenate([nbuf[m] for m in range(micro)], axis=1)
    grads = jnp.concatenate([dybuf[m] for m in range(micro)], axis=1)
    normed_low, normed_high = normed[:256], low_pad(normed[256:])
    grads_low, grads_high = grads[:256], high_pad(grads[256:])

    def weight_grads(g):
        rows = pl.ds(pl.multiple_of(g * block, 16), block)
        grad_pre = jnp.concatenate([gpre[m, rows, :] for m in range(micro)], axis=1)
        active = jnp.concatenate([hid[m, rows, :] for m in range(micro)], axis=1)
        up = nt(grad_pre, normed_low)
        down = nt(active, grads_low)
        mix = nt(grad_pre, normed_high) + nt(active, grads_high)
        for k in range(RING):
            r = slice(40 * k, 40 * k + 40)
            parts[g, k] = jnp.concatenate(
                [up[r, :128], up[r, 128:], down[r, :128], down[r, 128:], mix[r],
                 jnp.zeros((8, LANES), f32)], axis=0,
            ).astype(bf16)

    def write(result):
        both_out[0:40, 0:128] = result[0:40]
        both_out[0:40, 128:256] = result[40:80]
        both_out[0:40, 256:320] = result[160:200, 0:64]
        both_out[40:80, 0:128] = result[80:120]
        both_out[40:80, 128:256] = result[120:160]
        both_out[40:80, 256:320] = result[160:200, 64:128]

    def settle():
        @pl.when(s < last)
        def _():
            for m in range(micro):
                remote(obuf.at[m], xbuf.at[m], fs.at[m], fr.at[m], {"section": s + 1}).wait_send()

        @pl.when(s > 0)
        def _():
            for m in range(micro):
                remote(dsend.at[m], dybuf.at[m], bs.at[m], br.at[m], {"section": s - 1}).wait_send()

    @pl.when(sum_a)
    def _():
        sent = []
        sides = tuple(enumerate((1, -1)))

        def is_early(where):
            return where < (groups + 1) // 2

        def pass_on(i, side, where, distance, level, hops, add=None):
            g = (y_low + where) % groups
            k = (z + side * distance + RING) % RING
            source = parts.at[g, k]
            if add is not None:
                source = za.at[i, add, where]
                remote(source, source, zs.at[0], zr.at[i, add, where], at(y, z + 1)).wait_recv()
                source[...] = (source[...].astype(f32) + parts[g, k].astype(f32)).astype(bf16)
            copy = remote(
                source, za.at[i, level, where],
                zs.at[len(sent)], zr.at[i, level, where], at(y, z + side * hops),
            )
            copy.start()
            sent.append(copy)

        for where in range(groups):
            weight_grads((y_low + where) % groups)
            if far == 4:
                for i, side in sides:
                    if is_early(where) == (side == 1):
                        pass_on(i, side, where, 4, 0, 1)
                    else:
                        pass_on(i, side, where, 3, 1, 1)
        for where in range(groups):
            for i, side in sides:
                if far == 4 or is_early(where) == (side == 1):
                    pass_on(i, side, where, 1, far - 1, 1)
        if far == 4:
            for where in range(groups):
                for i, side in sides:
                    if is_early(where) == (side == 1):
                        pass_on(i, side, where, 3, 1, 1, add=0)
            for late in (True, False):
                for where in range(groups):
                    for i, side in sides:
                        if (is_early(where) != (side == 1)) == late:
                            pass_on(i, side, where, 2, 2, 2, add=1)
        for where in ((0, 2, 1, 3) if groups == 4 else range(groups)):
            g = (y_low + where) % groups
            total = parts[g, z].astype(f32)
            for i, side in sides:
                for level in ((2, 3) if far == 4 else (0,)):
                    if far == 1 and is_early(where) != (side == 1):
                        continue
                    source = za.at[i, level, where]
                    remote(source, source, zs.at[0], zr.at[i, level, where], at(y, z + 1)).wait_recv()
                    total += source[...].astype(f32)
            ysum[where] = total.astype(bf16)
            for e in range(1, height):
                if e % groups == where:
                    copy = remote(ysum.at[where], yall.at[y], ys.at[e], yr.at[y], at(y + e, z))
                    copy.start()
                    sent.append(copy)
        yall[y] = ysum[0]
        settle()
        for copy in sent:
            copy.wait_send()
        for e in range(1, height):
            source = yall.at[(y + e) % height]
            remote(source, source, ys.at[0], yr.at[(y + e) % height], at(y, z + 1)).wait_recv()
        total = yall[0].astype(f32)
        for e in range(1, height):
            total += yall[e].astype(f32)
        write(total)

    @pl.when(jnp.logical_not(sum_a))
    def _():
        sent = []
        far_first = [far] + [d for i in range(1, far) for d in (far - i, far + i)]
        if groups == 4:
            two = (y_low + 2) % groups
            weight_grads(two)
            for d in far_first + [0]:
                k = (z + d) % RING
                copy = remote(
                    parts.at[two, k], rh.at[k], rhs_.at[d], rhr.at[k],
                    at(y + jnp.where(k < far, -1, 1), z),
                )
                copy.start()
                sent.append(copy)
            for g in ((y_low + 1) % groups, (y_low + 3) % groups):
                weight_grads(g)

            def to_owner(d, relayed):
                k = (z + d) % RING
                side = jnp.where(k < far, 1, -1) * (-1 if relayed else 1)
                i = (1 - side) // 2
                g = (y_low + side + groups) % groups
                if relayed:
                    remote(rh.at[k], rh.at[k], rhs_.at[0], rhr.at[k], at(y, z + 1)).wait_recv()
                    parts[g, k] = (parts[g, k].astype(f32) + rh[k].astype(f32)).astype(bf16)
                copy = remote(
                    parts.at[g, k], ry.at[i, k], rys.at[1 if relayed else 0, d], ryr.at[i, k],
                    at(y + side, z),
                )
                copy.start()
                sent.append(copy)

            slots = far_first + [0]
            for d in slots[:far]:
                to_owner(d, False)
        weight_grads(y_low)
        if groups == 4:
            for i, d in enumerate(slots):
                to_owner(d, True)
                for later in slots[far + i : far + i + 1]:
                    to_owner(later, False)

        def group_sum(k):
            total = parts[y_low, k].astype(f32)
            if groups == 4:
                for i in range(2):
                    remote(ry.at[i, k], ry.at[i, k], rys.at[i, 0], ryr.at[i, k], at(y, z + 1)).wait_recv()
                total += ry[0, k].astype(f32) + ry[1, k].astype(f32)
            return total

        for d in far_first:
            k = (z + d) % RING
            qbuf[k] = group_sum(k).astype(bf16)
            copy = remote(qbuf.at[k], rz.at[d - 1], rzs.at[d - 1], rzr.at[d - 1], at(y, z + d))
            copy.start()
            sent.append(copy)
        result = group_sum(z)
        settle()
        for copy in sent:
            copy.wait_send()
        for d in range(1, RING):
            remote(rz.at[d - 1], rz.at[d - 1], rzs.at[0], rzr.at[d - 1], at(y, z + 1)).wait_recv()
            result += rz[d - 1].astype(f32)
        if tiles == 2:
            rounded = result.astype(bf16)
            tbuf[...] = rounded
            copy = remote(tbuf, rt, ts.at[0], tr.at[0], at(y + groups, z))
            copy.start()
            copy.wait()
            result = rounded.astype(f32) + rt[...].astype(f32)
        write(result)


def local(features, labels, w_expand, w_reduce, head_weight):
    sections, shards, tiles = (lax.axis_size(a) for a in ("section", "fsdp", "tile"))
    groups = shards // RING
    micro, rows, width = features.shape
    hidden = 40 * shards
    loss_scale = 1.0 / math.sqrt(micro * rows * shards * tiles)
    vmem, dma = pltpu.VMEM, pltpu.SemaphoreType.DMA
    half = RING // 2

    def body(*refs):
        kernel(sections, groups, tiles, micro, loss_scale, *refs)

    both = pl.pallas_call(
        body,
        out_shape=jax.ShapeDtypeStruct((80, width), f32),
        in_specs=[pl.BlockSpec(memory_space=pl.ANY)] * 5,
        out_specs=pl.BlockSpec(memory_space=pltpu.VMEM),
        scratch_shapes=[
            vmem((micro, width, rows), bf16),
            vmem((micro, rows), jnp.int32),
            vmem((40, width), bf16),
            vmem((40, width), bf16),
            vmem((5, width), bf16),
            vmem((shards, PACK, LANES), bf16),
            vmem((hidden, 256), bf16),
            vmem((hidden, 256), bf16),
            vmem((hidden, LANES), bf16),
            vmem((width, hidden), bf16),
            vmem((width, hidden), bf16),
            vmem((LANES, width), bf16),
            vmem((width, LANES), bf16),
            vmem((micro, width, rows), bf16),
            vmem((micro, width, rows), bf16),
            vmem((micro, width, rows), bf16),
            vmem((micro, width, rows), f32),
            vmem((micro, 1, rows), f32),
            vmem((micro, hidden, rows), f32),
            vmem((micro, hidden, rows), bf16),
            vmem((micro, hidden, rows), bf16),
            vmem((micro, width, rows), bf16),
            vmem((micro, width, rows), bf16),
            vmem((groups, RING, PACK, LANES), bf16),
            vmem((2, RING, PACK, LANES), bf16),
            vmem((RING, PACK, LANES), bf16),
            vmem((RING, PACK, LANES), bf16),
            vmem((RING - 1, PACK, LANES), bf16),
            vmem((PACK, LANES), bf16),
            vmem((PACK, LANES), bf16),
            vmem((2, half, groups, PACK, LANES), bf16),
            vmem((groups, PACK, LANES), bf16),
            vmem((groups * tiles, PACK, LANES), bf16),
            dma((5,)),
            dma((7 * RING,)),
            dma((shards, 2)),
            dma((micro,)),
            dma((micro,)),
            dma((micro,)),
            dma((micro,)),
            dma((2, RING)),
            dma((2, RING)),
            dma((RING,)),
            dma((RING,)),
            dma((RING - 1,)),
            dma((RING - 1,)),
            dma((1,)),
            dma((1,)),
            dma((groups * RING,)),
            dma((2, half, groups)),
            dma((groups * tiles,)),
            dma((groups * tiles,)),
        ],
        compiler_params=pltpu.CompilerParams(
            collective_id=0, has_side_effects=True, vmem_limit_bytes=60 * 1024 * 1024
        ),
    )(features.transpose(0, 2, 1), labels, w_expand[0].T, w_reduce[0].T, head_weight.T)
    return both[:40].T[None], both[40:].T[None]


def solution(mesh):
    return jax.shard_map(
        local,
        mesh=mesh,
        in_specs=(
            P(None, ("fsdp", "tile"), None),
            P(None, ("fsdp", "tile")),
            P("section", None, "fsdp"),
            P("section", None, "fsdp"),
            P(),
        ),
        out_specs=(P("section", None, "fsdp"), P("section", None, "fsdp")),
        check_vma=False,
    )
```

```python
import math

import jax
import jax.numpy as jnp
from jax import lax
from jax.experimental import pallas as pl
from jax.experimental.pallas import tpu as pltpu
from jax.sharding import PartitionSpec as P

norm_eps = 1e-06
RING = 8
LANES = 128
PACK = 208
HALF = 112
FIRST = 1
FIRST_SUM = 1
GELU_C = math.sqrt(2.0 / math.pi)
GELU_A = 0.044715
bf16 = jnp.bfloat16
f32 = jnp.float32


def nt(lhs, rhs):
    return lax.dot_general(lhs, rhs, (((1,), (1,)), ((), ())), preferred_element_type=f32)


def nn(lhs, rhs):
    return jnp.dot(lhs, rhs, preferred_element_type=f32)


def eye(size):
    row = lax.broadcasted_iota(jnp.int32, (size, size), 0)
    column = lax.broadcasted_iota(jnp.int32, (size, size), 1)
    return jnp.where(row == column, 1.0, 0.0).astype(bf16)


def place(shift):
    row = lax.broadcasted_iota(jnp.int32, (LANES, 64), 0)
    column = lax.broadcasted_iota(jnp.int32, (LANES, 64), 1)
    return jnp.where(row == column + shift, 1.0, 0.0).astype(bf16)


def normalize(values):
    floats = values.astype(f32)
    centred = floats - jnp.mean(floats, axis=0, keepdims=True)
    inverse_std = lax.rsqrt(jnp.mean(centred * centred, axis=0, keepdims=True) + norm_eps)
    return centred * inverse_std, inverse_std


def norm_back(unit, inverse_std, grad):
    centred = grad - jnp.mean(grad, axis=0, keepdims=True)
    return inverse_std * (centred - unit * jnp.mean(grad * unit, axis=0, keepdims=True))


def low_pad(rows):
    return jnp.concatenate([rows, jnp.zeros_like(rows)], axis=0)


def high_pad(rows):
    return jnp.concatenate([jnp.zeros_like(rows), rows], axis=0)


def remote(src, dst, send_sem, recv_sem, device):
    return pltpu.make_async_remote_copy(
        src_ref=src,
        dst_ref=dst,
        send_sem=send_sem,
        recv_sem=recv_sem,
        device_id=device,
        device_id_type=pl.DeviceIdType.MESH,
    )


def kernel(
    sections, groups, tiles, micro, loss_scale,
    feat_any, labels_any, wup_any, wdown_any, head_any,
    both_out,
    feat, labels, wup, wdown, head, gathered, up_t, down_t, mix_t, up_n, down_n, head_pad, head_n,
    xbuf, obuf, nbuf, ubuf, istd, pre, hid, gpre, dybuf, dsend,
    parts, ry, rh, qbuf, rz, tbuf, rt, za, ysum, yall,
    in_sem, g_s, g_r, fs, fr, bs, br, rys, ryr, rhs_, rhr, rzs, rzr, ts, tr, zs, zr, ys, yr,
):
    s = lax.axis_index("section")
    f = lax.axis_index("fsdp")
    t = lax.axis_index("tile")
    y_low, z = f // RING, f % RING
    height = groups * tiles
    y = t * groups + y_low
    last = sections - 1
    block = 40 * RING
    hidden = block * groups
    fine = math.gcd(hidden, 128)

    def at(y_new, z_new):
        y_new = (y_new + 2 * height) % height
        z_new = (z_new + 2 * RING) % RING
        return {"fsdp": (y_new % groups) * RING + z_new, "tile": y_new // groups}

    copies_in = [
        pltpu.make_async_copy(source, target, in_sem.at[i])
        for i, (source, target) in enumerate(
            ((wup_any, wup), (wdown_any, wdown), (feat_any, feat), (labels_any, labels), (head_any, head))
        )
    ]
    for copy in copies_in:
        copy.start()

    barrier = pltpu.get_barrier_semaphore()
    def near(size):
        return (1, -1, 2, -2) if size > 4 else range(1, size)

    partners = [at(y, z + d) for d in near(RING)] + [at(y + d, z) for d in near(height)]
    for device in partners:
        pl.semaphore_signal(barrier, inc=1, device_id=device, device_id_type=pl.DeviceIdType.MESH)

    @pl.when(s > 0)
    def _():
        pl.semaphore_signal(
            barrier, inc=1, device_id={"section": s - 1}, device_id_type=pl.DeviceIdType.MESH
        )

    @pl.when(s < last)
    def _():
        pl.semaphore_signal(
            barrier, inc=1, device_id={"section": s + 1}, device_id_type=pl.DeviceIdType.MESH
        )

    for copy in copies_in[:2]:
        copy.wait()
    up_w, down_w = wup[...], wdown[...]
    mixed = nt(up_w[:, 256:], place(0)) + nt(down_w[:, 256:], place(64))
    pieces = [up_w[:, :128], up_w[:, 128:256], down_w[:, :128], down_w[:, 128:256]]
    pieces = [piece.astype(f32) for piece in pieces] + [mixed, jnp.zeros((8, LANES), f32)]
    gathered[f] = jnp.concatenate(pieces, axis=0).astype(bf16)

    pl.semaphore_wait(
        barrier,
        len(partners) + jnp.where(s > 0, 1, 0) + jnp.where(s < last, 1, 0),
    )

    def slot(j, dz):
        return ((y_low + j) % groups) * RING + (z + dz + 2 * RING) % RING

    order = (0, 1, 3, 2) if groups == 4 else (0,)
    far = RING // 2
    low_rows, high_rows = pl.ds(0, HALF), pl.ds(HALF, PACK - HALF)
    is_a = s % 2 == FIRST
    sum_a = s % 2 == FIRST_SUM

    def arrived(index):
        remote(
            gathered.at[index], gathered.at[index], g_s.at[0], g_r.at[index, 0], at(y, z + 1)
        ).wait_recv()

    def halves_arrived(index):
        for i, rows in enumerate((low_rows, high_rows)):
            remote(
                gathered.at[index, rows], gathered.at[index, rows],
                g_s.at[0], g_r.at[index, i], at(y, z + 1),
            ).wait_recv()

    def y_sends(index, first):
        if groups != 4:
            return []
        copies = [
            remote(gathered.at[index], gathered.at[index], g_s.at[first], g_r.at[index, 0], at(y + 1, z)),
            remote(gathered.at[index], gathered.at[index], g_s.at[first + 1], g_r.at[index, 0], at(y - 1, z)),
            remote(
                gathered.at[index, low_rows], gathered.at[index, low_rows],
                g_s.at[first + 2], g_r.at[index, 0], at(y + 2, z),
            ),
            remote(
                gathered.at[index, high_rows], gathered.at[index, high_rows],
                g_s.at[first + 3], g_r.at[index, 1], at(y - 2, z),
            ),
        ]
        for copy in copies:
            copy.start()
        return copies

    def unpack(pair, carry):
        first = gathered[2 * pair].astype(f32)
        second = gathered[2 * pair + 1].astype(f32)
        rows = pl.ds(pl.multiple_of(pair * 80, 16), 80)

        def both(i):
            return jnp.concatenate(
                [first[40 * i : 40 * i + 40], second[40 * i : 40 * i + 40]], axis=0
            ).astype(bf16)

        up_t[rows, 0:128] = both(0)
        up_t[rows, 128:256] = both(1)
        down_t[rows, 0:128] = both(2)
        down_t[rows, 128:256] = both(3)
        mix_t[rows, :] = both(4)
        return carry

    pairs = RING // 2
    soon, late = ((0, 1, 3), 2) if far == 4 else ((), 0)

    def take_inputs():
        for copy in copies_in[2:]:
            copy.wait()

        @pl.when(s == 0)
        def _():
            for m in range(micro):
                xbuf[m] = feat[m]

    def unpack_column(r):
        def one(j, carry):
            return unpack((y_low + j) % groups * pairs + (z // 2 + r) % pairs, carry)

        lax.fori_loop(0, groups, one, 0, unroll=r == late)

    @pl.when(is_a)
    def _():
        sent = y_sends(f, 0)

        def z_send(index, d):
            copy = remote(
                gathered.at[index], gathered.at[index],
                g_s.at[len(sent)], g_r.at[index, 0], at(y, z + d),
            )
            copy.start()
            sent.append(copy)

        def is_early(j):
            return j in order[: (len(order) + 1) // 2]

        def spread(j):
            for side in (1, -1):
                if far > 1 or is_early(j) == (side == 1):
                    z_send(slot(j, 0), side)

        def forward_from(j, distance):
            for side in (1, -1):
                index = slot(j, -side * distance)
                arrived(index)
                if distance + 1 < far or is_early(j) == (side == 1):
                    z_send(index, side)

        spread(0)
        for j in order[1:3]:
            arrived(slot(j, 0))
            spread(j)
        if far > 1:
            forward_from(0, 1)
        if len(order) > 3:
            halves_arrived(slot(2, 0))
            spread(2)
        if far > 1:
            for j in order[1:]:
                forward_from(j, 1)
        if far > 2:
            for distance in (2, 3):
                for j in (0,) + order[1:]:
                    forward_from(j, distance)
        for r in soon:
            unpack_column(r)
        take_inputs()
        for copy in sent:
            copy.wait_send()
        for j in order:
            arrived(slot(j, far))
        unpack_column(late)

    near_first = [d for i in range(1, far) for d in (i, -i)] + [far]

    @pl.when(jnp.logical_not(is_a))
    def _():
        sent = []

        def z_send(index, d, rows=None, half=0):
            ref = gathered.at[index] if rows is None else gathered.at[index, rows]
            copy = remote(ref, ref, g_s.at[len(sent)], g_r.at[index, half], at(y, z + d))
            copy.start()
            sent.append(copy)

        for d in (2, -2, 1, -1) if far == 4 else near_first:
            z_send(f, d)
        sent += y_sends(f, len(sent))
        if far == 4:
            for side in (1, -1):
                index = slot(0, -2 * side)
                arrived(index)
                z_send(index, side)
                z_send(index, 2 * side, low_rows if side == 1 else high_rows, 0 if side == 1 else 1)
        for d in near_first:
            index = slot(0, d)
            if abs(d) == 4:
                halves_arrived(index)
            elif abs(d) != 2:
                arrived(index)
            sent += y_sends(index, len(sent))
        for r in soon + (late,):
            if r == late:
                take_inputs()
                for copy in sent:
                    copy.wait_send()
            if groups == 4:
                first = (z // 2 + r) % pairs * 2
                for j in (1, 3, 2):
                    for index in (first, first + 1):
                        index += (y_low + j) % groups * RING
                        (halves_arrived if j == 2 else arrived)(index)
            unpack_column(r)

    wide = eye(256)
    down_n[0:256, :] = nt(wide, down_t[...]).astype(bf16)
    turned = nt(eye(128), mix_t[...]).astype(bf16)
    down_n[256:320, :] = turned[64:128]

    @pl.when(s > 0)
    def _():
        up_n[0:256, :] = nt(wide, up_t[...]).astype(bf16)
        up_n[256:320, :] = turned[0:64]

    @pl.when(s == last)
    def _():
        head_pad[...] = jnp.zeros_like(head_pad)
        head_pad[0:5, :] = head[...]
        head_n[...] = nt(eye(320), head_pad[...]).astype(bf16)

    def forward(m, carry):
        @pl.when(s > 0)
        def _():
            remote(obuf.at[m], xbuf.at[m], fs.at[m], fr.at[m], {"section": s}).wait_recv()

        x = xbuf[m]
        unit, inverse_std = normalize(x)
        normed = unit.astype(bf16)
        ubuf[m] = unit
        istd[m] = inverse_std
        nbuf[m] = normed
        low, high = normed[:256], low_pad(normed[256:])
        total = x.astype(f32)
        active = []
        for first in range(0, hidden, fine):
            rows = slice(first, first + fine)
            before = nn(up_t[rows, :], low) + nn(mix_t[rows, :], high)
            pre[m, rows, :] = before
            bent = jnp.tanh(GELU_C * (before + GELU_A * (before * before * before)))
            active.append((before * (0.5 * (1.0 + bent))).astype(bf16))
            hid[m, rows, :] = active[-1]
        out = (total + nn(down_n[...], jnp.concatenate(active, axis=0))).astype(bf16)
        obuf[m] = out

        @pl.when(s < last)
        def _():
            remote(obuf.at[m], xbuf.at[m], fs.at[m], fr.at[m], {"section": s + 1}).start()

        return carry

    lax.fori_loop(0, micro, forward, 0)

    @pl.when(s == last)
    def _():
        for m in range(micro):
            head_unit, head_istd = normalize(obuf[m])
            logits = nn(head_pad[0:16, :], head_unit.astype(bf16))[0:8]
            classes = lax.broadcasted_iota(jnp.int32, logits.shape, 0)
            exponent = jnp.where(classes < 5, jnp.exp(logits), 0.0)
            probs = exponent / jnp.sum(exponent, axis=0, keepdims=True)
            onehot = jnp.where(classes == labels[m : m + 1, :], 1.0, 0.0)
            grad_logits = (probs - onehot) * loss_scale
            grad_logits = jnp.concatenate(
                [grad_logits, jnp.zeros((LANES - 8, LANES), f32)], axis=0
            ).astype(bf16)
            grad_norm = nn(head_n[...], grad_logits)
            dybuf[m] = norm_back(head_unit, head_istd, grad_norm).astype(bf16)

    def backward(m, carry):
        @pl.when(s < last)
        def _():
            remote(dsend.at[m], dybuf.at[m], bs.at[m], br.at[m], {"section": s}).wait_recv()

        dy = dybuf[m]
        low, high = dy[:256], high_pad(dy[256:])
        for first in range(0, hidden, fine // 2):
            rows = slice(first, first + fine // 2)
            grad_hidden = nn(down_t[rows, :], low) + nn(mix_t[rows, :], high)
            before = pre[m, rows, :]
            square = before * before
            bent = jnp.tanh(before * (GELU_C + (GELU_C * GELU_A) * square))
            share = 0.5 + 0.5 * bent
            slope = share + (share * (1.0 - bent)) * (
                before * (GELU_C + (3.0 * GELU_C * GELU_A) * square)
            )
            gpre[m, rows, :] = (grad_hidden * slope).astype(bf16)

        @pl.when(s > 0)
        def _():
            grad_norm = nn(up_n[...], gpre[m])
            grad_in = dybuf[m].astype(f32) + norm_back(ubuf[m], istd[m], grad_norm)
            dsend[m] = grad_in.astype(bf16)
            remote(dsend.at[m], dybuf.at[m], bs.at[m], br.at[m], {"section": s - 1}).start()

        return carry

    lax.fori_loop(0, micro, backward, 0)

    normed = jnp.concatenate([nbuf[m] for m in range(micro)], axis=1)
    grads = jnp.concatenate([dybuf[m] for m in range(micro)], axis=1)
    normed_low, normed_high = normed[:256], low_pad(normed[256:])
    grads_low, grads_high = grads[:256], high_pad(grads[256:])

    def weight_grads(g):
        rows = pl.ds(pl.multiple_of(g * block, 16), block)
        grad_pre = jnp.concatenate([gpre[m, rows, :] for m in range(micro)], axis=1)
        active = jnp.concatenate([hid[m, rows, :] for m in range(micro)], axis=1)
        up = nt(grad_pre, normed_low)
        down = nt(active, grads_low)
        mix = nt(grad_pre, normed_high) + nt(active, grads_high)
        for k in range(RING):
            r = slice(40 * k, 40 * k + 40)
            parts[g, k] = jnp.concatenate(
                [up[r, :128], up[r, 128:], down[r, :128], down[r, 128:], mix[r],
                 jnp.zeros((8, LANES), f32)], axis=0,
            ).astype(bf16)

    def write(result):
        both_out[0:40, 0:128] = result[0:40]
        both_out[0:40, 128:256] = result[40:80]
        both_out[0:40, 256:320] = result[160:200, 0:64]
        both_out[40:80, 0:128] = result[80:120]
        both_out[40:80, 128:256] = result[120:160]
        both_out[40:80, 256:320] = result[160:200, 64:128]

    def settle():
        @pl.when(s < last)
        def _():
            for m in range(micro):
                remote(obuf.at[m], xbuf.at[m], fs.at[m], fr.at[m], {"section": s + 1}).wait_send()

        @pl.when(s > 0)
        def _():
            for m in range(micro):
                remote(dsend.at[m], dybuf.at[m], bs.at[m], br.at[m], {"section": s - 1}).wait_send()

    @pl.when(sum_a)
    def _():
        sent = []
        sides = tuple(enumerate((1, -1)))

        def is_early(where):
            return where < (groups + 1) // 2

        def pass_on(i, side, where, distance, level, hops, add=None):
            g = (y_low + where) % groups
            k = (z + side * distance + RING) % RING
            source = parts.at[g, k]
            if add is not None:
                source = za.at[i, add, where]
                remote(source, source, zs.at[0], zr.at[i, add, where], at(y, z + 1)).wait_recv()
                source[...] = (source[...].astype(f32) + parts[g, k].astype(f32)).astype(bf16)
            copy = remote(
                source, za.at[i, level, where],
                zs.at[len(sent)], zr.at[i, level, where], at(y, z + side * hops),
            )
            copy.start()
            sent.append(copy)

        for where in range(groups):
            weight_grads((y_low + where) % groups)
            if far == 4:
                for i, side in sides:
                    if is_early(where) == (side == 1):
                        pass_on(i, side, where, 4, 0, 1)
                    else:
                        pass_on(i, side, where, 3, 1, 1)
        for where in range(groups):
            for i, side in sides:
                if far == 4 or is_early(where) == (side == 1):
                    pass_on(i, side, where, 1, far - 1, 1)
        if far == 4:
            for where in range(groups):
                for i, side in sides:
                    if is_early(where) == (side == 1):
                        pass_on(i, side, where, 3, 1, 1, add=0)
            for late in (True, False):
                for where in range(groups):
                    for i, side in sides:
                        if (is_early(where) != (side == 1)) == late:
                            pass_on(i, side, where, 2, 2, 2, add=1)
        for where in ((0, 2, 1, 3) if groups == 4 else range(groups)):
            g = (y_low + where) % groups
            total = parts[g, z].astype(f32)
            for i, side in sides:
                for level in ((2, 3) if far == 4 else (0,)):
                    if far == 1 and is_early(where) != (side == 1):
                        continue
                    source = za.at[i, level, where]
                    remote(source, source, zs.at[0], zr.at[i, level, where], at(y, z + 1)).wait_recv()
                    total += source[...].astype(f32)
            ysum[where] = total.astype(bf16)
            for e in range(1, height):
                if e % groups == where:
                    copy = remote(ysum.at[where], yall.at[y], ys.at[e], yr.at[y], at(y + e, z))
                    copy.start()
                    sent.append(copy)
        yall[y] = ysum[0]
        settle()
        for copy in sent:
            copy.wait_send()
        for e in range(1, height):
            source = yall.at[(y + e) % height]
            remote(source, source, ys.at[0], yr.at[(y + e) % height], at(y, z + 1)).wait_recv()
        total = yall[0].astype(f32)
        for e in range(1, height):
            total += yall[e].astype(f32)
        write(total)

    @pl.when(jnp.logical_not(sum_a))
    def _():
        sent = []
        far_first = [far] + [d for i in range(1, far) for d in (far - i, far + i)]
        if groups == 4:
            two = (y_low + 2) % groups
            weight_grads(two)
            for d in far_first + [0]:
                k = (z + d) % RING
                copy = remote(
                    parts.at[two, k], rh.at[k], rhs_.at[d], rhr.at[k],
                    at(y + jnp.where(k < far, -1, 1), z),
                )
                copy.start()
                sent.append(copy)
            for g in ((y_low + 1) % groups, (y_low + 3) % groups):
                weight_grads(g)

            def to_owner(d, relayed):
                k = (z + d) % RING
                side = jnp.where(k < far, 1, -1) * (-1 if relayed else 1)
                i = (1 - side) // 2
                g = (y_low + side + groups) % groups
                if relayed:
                    remote(rh.at[k], rh.at[k], rhs_.at[0], rhr.at[k], at(y, z + 1)).wait_recv()
                    parts[g, k] = (parts[g, k].astype(f32) + rh[k].astype(f32)).astype(bf16)
                copy = remote(
                    parts.at[g, k], ry.at[i, k], rys.at[1 if relayed else 0, d], ryr.at[i, k],
                    at(y + side, z),
                )
                copy.start()
                sent.append(copy)

            slots = far_first + [0]
            for d in slots[:far]:
                to_owner(d, False)
        weight_grads(y_low)
        if groups == 4:
            for i, d in enumerate(slots):
                to_owner(d, True)
                for later in slots[far + i : far + i + 1]:
                    to_owner(later, False)

        def group_sum(k):
            total = parts[y_low, k].astype(f32)
            if groups == 4:
                for i in range(2):
                    remote(ry.at[i, k], ry.at[i, k], rys.at[i, 0], ryr.at[i, k], at(y, z + 1)).wait_recv()
                total += ry[0, k].astype(f32) + ry[1, k].astype(f32)
            return total

        for d in far_first:
            k = (z + d) % RING
            qbuf[k] = group_sum(k).astype(bf16)
            copy = remote(qbuf.at[k], rz.at[d - 1], rzs.at[d - 1], rzr.at[d - 1], at(y, z + d))
            copy.start()
            sent.append(copy)
        result = group_sum(z)
        settle()
        for copy in sent:
            copy.wait_send()
        for d in range(1, RING):
            remote(rz.at[d - 1], rz.at[d - 1], rzs.at[0], rzr.at[d - 1], at(y, z + 1)).wait_recv()
            result += rz[d - 1].astype(f32)
        if tiles == 2:
            rounded = result.astype(bf16)
            tbuf[...] = rounded
            copy = remote(tbuf, rt, ts.at[0], tr.at[0], at(y + groups, z))
            copy.start()
            copy.wait()
            result = rounded.astype(f32) + rt[...].astype(f32)
        write(result)


def local(features, labels, w_expand, w_reduce, head_weight):
    sections, shards, tiles = (lax.axis_size(a) for a in ("section", "fsdp", "tile"))
    groups = shards // RING
    micro, rows, width = features.shape
    hidden = 40 * shards
    loss_scale = 1.0 / math.sqrt(micro * rows * shards * tiles)
    vmem, dma = pltpu.VMEM, pltpu.SemaphoreType.DMA
    half = RING // 2

    def body(*refs):
        kernel(sections, groups, tiles, micro, loss_scale, *refs)

    both = pl.pallas_call(
        body,
        out_shape=jax.ShapeDtypeStruct((80, width), f32),
        in_specs=[pl.BlockSpec(memory_space=pl.ANY)] * 5,
        out_specs=pl.BlockSpec(memory_space=pltpu.VMEM),
        scratch_shapes=[
            vmem((micro, width, rows), bf16),
            vmem((micro, rows), jnp.int32),
            vmem((40, width), bf16),
            vmem((40, width), bf16),
            vmem((5, width), bf16),
            vmem((shards, PACK, LANES), bf16),
            vmem((hidden, 256), bf16),
            vmem((hidden, 256), bf16),
            vmem((hidden, LANES), bf16),
            vmem((width, hidden), bf16),
            vmem((width, hidden), bf16),
            vmem((LANES, width), bf16),
            vmem((width, LANES), bf16),
            vmem((micro, width, rows), bf16),
            vmem((micro, width, rows), bf16),
            vmem((micro, width, rows), bf16),
            vmem((micro, width, rows), f32),
            vmem((micro, 1, rows), f32),
            vmem((micro, hidden, rows), f32),
            vmem((micro, hidden, rows), bf16),
            vmem((micro, hidden, rows), bf16),
            vmem((micro, width, rows), bf16),
            vmem((micro, width, rows), bf16),
            vmem((groups, RING, PACK, LANES), bf16),
            vmem((2, RING, PACK, LANES), bf16),
            vmem((RING, PACK, LANES), bf16),
            vmem((RING, PACK, LANES), bf16),
            vmem((RING - 1, PACK, LANES), bf16),
            vmem((PACK, LANES), bf16),
            vmem((PACK, LANES), bf16),
            vmem((2, half, groups, PACK, LANES), bf16),
            vmem((groups, PACK, LANES), bf16),
            vmem((groups * tiles, PACK, LANES), bf16),
            dma((5,)),
            dma((7 * RING,)),
            dma((shards, 2)),
            dma((micro,)),
            dma((micro,)),
            dma((micro,)),
            dma((micro,)),
            dma((2, RING)),
            dma((2, RING)),
            dma((RING,)),
            dma((RING,)),
            dma((RING - 1,)),
            dma((RING - 1,)),
            dma((1,)),
            dma((1,)),
            dma((groups * RING,)),
            dma((2, half, groups)),
            dma((groups * tiles,)),
            dma((groups * tiles,)),
        ],
        compiler_params=pltpu.CompilerParams(
            collective_id=0, has_side_effects=True, vmem_limit_bytes=60 * 1024 * 1024
        ),
    )(features.transpose(0, 2, 1), labels, w_expand[0].T, w_reduce[0].T, head_weight.T)
    return both[:40].T[None], both[40:].T[None]


def solution(mesh):
    return jax.shard_map(
        local,
        mesh=mesh,
        in_specs=(
            P(None, ("fsdp", "tile"), None),
            P(None, ("fsdp", "tile")),
            P("section", None, "fsdp"),
            P("section", None, "fsdp"),
            P(),
        ),
        out_specs=(P("section", None, "fsdp"), P("section", None, "fsdp")),
        check_vma=False,
    )
```
